512 devices in a mesh: worker: 64 (over y, z), tensor: 8 (over x, core).
Axes of the slice: x: 4, y: 8, z: 8, core: 2. Of those that a mesh axis runs over, the one named last changes fastest.
Arguments:
- queries: bfloat16 [256, 256, 1024], P('worker', None, 'tensor'), may hold values from -6 to 6
- key_heads: bfloat16 [256, 256, 1024], P('worker', None, 'tensor'), may hold values from -6 to 6
- values_in: bfloat16 [256, 256, 2048], P('worker', None, 'tensor'), may hold values from -6 to 6
- out_gate: bfloat16 [256, 256, 2048], P('worker', None, 'tensor'), may hold values from -6 to 6
- log_decay: float32 [256, 16, 256], P('worker', 'tensor'), may hold values from -1 to 0
- write_rate: float32 [256, 16, 256], P('worker', 'tensor'), may hold values from 0.5 to 0.95
- cache_states: float32 [768, 16, 128, 128], P('worker', 'tensor'), may hold values from -6 to 6
- norm_gain: float32 [128], replicated, may hold values from 0.1 to 1.9
- out_proj: bfloat16 [2048, 2048], P('tensor'), may hold values from -0.125 to 0.125
- hit_owner: int32 [256], P('worker'), may hold values from 0 to 63, as said below
- hit_node: int32 [256], P('worker'), may hold values from 0 to 11
- prefix_len: int32 [256], P('worker'), may hold values from 0 to 768, as said below
- write_slot: int32 [256], P('worker'), may hold values from 0 to 255, as said below
Outputs:
- mixed: bfloat16 [256, 256, 2048], P('worker', None, 'tensor')
- end_states: float32 [256, 16, 128, 128], P('worker', 'tensor')
The draws below stay inside these ranges and needn't reach their ends.
Inputs may be any that keep to these rules, and one draw needn't show every extreme that they name: `hit_owner`: the worker at most 2 positions away from the request's own worker along the worker axis, counted around the end (the first worker follows the last); all of one worker's requests may name workers at the same distance. `prefix_len`: a multiple of 256; 0 where nothing is cached, and hit_owner and hit_node are then unused. A permutation of 0 to 255; row write_slot[r] lies on worker write_slot[r] // 4, at most 2 positions away from request r's worker, counted around the end.
All inputs are finite; a program needn't handle non-finite values.
Results may differ from the reference program's by a relative error of at most 0.017.
Values may be sent and summed in bfloat16 or wider, within the bound.
A program may use at most 64 MiB of HBM per device.

```python
import jax
import jax.numpy as jnp
from jax import lax

D = 2048
VALUE_HEAD_HALF = 16
HK = 8
DK = 128
DV = 128
NEW_TOKENS = 256
REACH = 2
REQ_DEV = 4
CACHE_DEV = 12
REQUEST_TOTAL = 256
SLOTS = 768
N_TENSOR = 8


def request_plan(key):
    worker_count = REQUEST_TOTAL // REQ_DEV
    random_child_keys = jax.random.split(key, 5)
    worker = jnp.arange(REQUEST_TOTAL, dtype=jnp.int32) // REQ_DEV
    offsets = jax.random.randint(random_child_keys[0], (REQUEST_TOTAL,), -REACH, REACH + 1)
    full_worker = jax.random.randint(random_child_keys[1], (), 0, worker_count)
    direction = 2 * jax.random.randint(random_child_keys[2], (), 0, 2) - 1
    full_offset = direction * jax.random.randint(random_child_keys[3], (), 1, REACH + 1)
    offsets = jnp.where(worker == full_worker, full_offset, offsets)
    far_right = (full_worker + worker_count // 2) % worker_count * REQ_DEV
    far_left = (full_worker + worker_count // 2 + 1) % worker_count * REQ_DEV
    offsets = offsets.at[far_right].set(REACH).at[far_left].set(-REACH)
    owner_ids = (worker + offsets + worker_count) % worker_count
    request_ids = jnp.arange(REQUEST_TOTAL, dtype=jnp.int32)
    spans_cached = jax.random.randint(random_child_keys[4], (REQUEST_TOTAL,), 0, 4)
    forced = (worker == full_worker) | (request_ids == far_right) | (request_ids == far_left)
    spans_cached = jnp.where(forced, jnp.maximum(spans_cached, 1), spans_cached)
    spans_cached = spans_cached.at[far_right].set(3)
    return (owner_ids.astype(jnp.int32), (spans_cached * NEW_TOKENS).astype(jnp.int32))


def draw_hit_owner(key, part):
    owner_ids, prefix_lengths = request_plan(key)
    return owner_ids


def draw_prefix_len(key, part):
    owner_ids, prefix_lengths = request_plan(key)
    return prefix_lengths


def lane_order(order_key):
    return jax.random.permutation(order_key, REQ_DEV).astype(jnp.int32)


def draw_write_slot(key, part):
    key = jax.random.fold_in(key, 7)
    worker_count = REQUEST_TOTAL // REQ_DEV
    lane_ids = jnp.arange(REQ_DEV, dtype=jnp.int32)
    pair_ids = jnp.arange(worker_count // 2, dtype=jnp.int32)
    destination = jnp.arange(REQUEST_TOTAL, dtype=jnp.int32)
    for round_index in range(REACH):
        round_key = jax.random.fold_in(key, round_index)
        bit_key, order_key = jax.random.split(round_key)
        swap_bits = jax.random.randint(bit_key, (worker_count // 2, REQ_DEV), 0, 2)
        swap_bits = swap_bits.at[0].set(1)
        orders = jax.vmap(lane_order)(jax.random.split(order_key, worker_count // 2))
        left_worker = (2 * pair_ids + round_index % 2) % worker_count
        right_worker = (2 * pair_ids + 1 + round_index % 2) % worker_count
        left_slots = left_worker[:, None] * REQ_DEV + lane_ids[None, :]
        right_slots = right_worker[:, None] * REQ_DEV + orders
        mapping = jnp.arange(REQUEST_TOTAL, dtype=jnp.int32)
        mapping = mapping.at[left_slots].set(jnp.where(swap_bits > 0, right_slots, left_slots))
        mapping = mapping.at[right_slots].set(jnp.where(swap_bits > 0, left_slots, right_slots))
        destination = mapping[destination]
    return destination.astype(jnp.int32)


def draw_key_heads(key, part):
    key = jax.random.fold_in(key, 13)
    shared_key, noise_key = jax.random.split(key)
    shared = jax.random.normal(shared_key, (REQUEST_TOTAL, 1, HK, DK), jnp.float32)
    noise = 0.3 * jax.random.normal(noise_key, (REQUEST_TOTAL, NEW_TOKENS, HK, DK), jnp.float32)
    rows = jnp.clip(shared + noise, -6.0, 6.0)
    return rows.reshape(REQUEST_TOTAL, NEW_TOKENS, HK * DK).astype(jnp.bfloat16)


def draw_log_decay(key, part):
    key = jax.random.fold_in(key, 11)
    random_child_keys = jax.random.split(key, 6)
    fast_share = 0.5
    slow_low = 0.1
    slow_high = 0.6
    fast_heads = jax.random.bernoulli(random_child_keys[0], fast_share, (REQUEST_TOTAL, VALUE_HEAD_HALF, 1))
    slow_rate = jnp.exp(jax.random.uniform(random_child_keys[1], (REQUEST_TOTAL, VALUE_HEAD_HALF, 1), jnp.float32, jnp.log(slow_low), jnp.log(slow_high))) / NEW_TOKENS
    fast_rate = 2.3 / jax.random.uniform(random_child_keys[2], (REQUEST_TOTAL, VALUE_HEAD_HALF, 1), jnp.float32, 30.0, 50.0)
    baseline_rate = jnp.where(fast_heads, fast_rate, slow_rate)
    random_wobble = jnp.exp(jax.random.uniform(random_child_keys[3], (REQUEST_TOTAL, VALUE_HEAD_HALF, NEW_TOKENS), jnp.float32, -0.7, 0.7))
    spike_events = jax.random.bernoulli(random_child_keys[4], 2.0 / NEW_TOKENS, (REQUEST_TOTAL, VALUE_HEAD_HALF, NEW_TOKENS))
    spike_penalty = jax.random.uniform(random_child_keys[5], (REQUEST_TOTAL, VALUE_HEAD_HALF, NEW_TOKENS), jnp.float32, 0.22, 0.69)
    return -(baseline_rate * random_wobble + jnp.where(spike_events, spike_penalty, 0.0))


def with_ends(values, key, least, top_value):
    longest = values.shape.index(max(values.shape))
    spots = []
    for shift in (0, 1):
        where = [jax.random.randint(jax.random.fold_in(key, axis), (), 0, length) for axis, length in enumerate(values.shape)]
        where[longest] = (where[longest] + shift) % values.shape[longest]
        spots.append(tuple(where))
    return values.at[spots[0]].set(least).at[spots[1]].set(top_value)


def block_scale(own_key, dims, cuts, low, high):
    level, own = 1.0, jax.random.fold_in(own_key, 6)
    for dim, parts in cuts:
        steps = jnp.exp(jax.random.uniform(jax.random.fold_in(own, dim), (parts,), jnp.float32, low / len(cuts), high / len(cuts)))
        level = level * jnp.repeat(steps, dims[dim] // parts).reshape([-1 if axis == dim else 1 for axis in range(len(dims))])
    return level


def bell_draw(key, dims, scale, reach, pieces=(), kind=jnp.bfloat16):
    entries = scale * jax.random.normal(key, dims, jnp.float32)
    if pieces:
        entries = entries * block_scale(key, dims, pieces, -0.22, 0.18)
    return jnp.clip(entries, -reach, reach).astype(kind)


def setup_inputs(seed: int = 0) -> dict:
    splits = jax.random.split(jax.random.key(seed), 14)
    queries = bell_draw(splits[0], (REQUEST_TOTAL, NEW_TOKENS, HK * DK), 1.0, 6.0, ((0, 64), (2, 8)))
    key_heads = draw_key_heads(jax.random.fold_in(splits[13], 71), 0)
    values_in = bell_draw(splits[2], (REQUEST_TOTAL, NEW_TOKENS, VALUE_HEAD_HALF * DV), 1.0, 6.0, ((0, 64), (2, 8)))
    out_gate = bell_draw(splits[3], (REQUEST_TOTAL, NEW_TOKENS, VALUE_HEAD_HALF * DV), 1.0, 6.0, ((0, 64), (2, 8)))
    log_decay = draw_log_decay(jax.random.fold_in(splits[13], 71), 0)
    write_rate = jnp.clip(0.5 + 0.45 * jax.random.uniform(splits[5], (REQUEST_TOTAL, VALUE_HEAD_HALF, NEW_TOKENS), jnp.float32) ** block_scale(splits[5], (REQUEST_TOTAL, VALUE_HEAD_HALF, NEW_TOKENS), ((0, 64), (1, 8)), -0.2, 0.2), 0.5, 0.95)
    cache_states = bell_draw(splits[6], (SLOTS, VALUE_HEAD_HALF, DK, DV), 1.0, 6.0, ((0, 64), (1, 8)), jnp.float32)
    norm_gain = jnp.clip(1.0 + 0.18 * jax.random.normal(splits[7], (DV,), jnp.float32), 0.1, 1.9)
    out_proj = bell_draw(splits[8], (VALUE_HEAD_HALF * DV, D), (VALUE_HEAD_HALF * DV) ** -0.5, 0.125, ((0, 8),))
    hit_owner = draw_hit_owner(jax.random.fold_in(splits[13], 71), 0)
    hit_node = with_ends(jax.random.randint(splits[10], (REQUEST_TOTAL,), 0, CACHE_DEV), jax.random.fold_in(splits[10], 1), 0, CACHE_DEV - 1).astype(jnp.int32)
    prefix_len = draw_prefix_len(jax.random.fold_in(splits[13], 71), 0)
    write_slot = draw_write_slot(jax.random.fold_in(splits[13], 71), 0)
    return dict(queries=queries, key_heads=key_heads, values_in=values_in, out_gate=out_gate, log_decay=log_decay, write_rate=write_rate, cache_states=cache_states, norm_gain=norm_gain, out_proj=out_proj, hit_owner=hit_owner, hit_node=hit_node, prefix_len=prefix_len, write_slot=write_slot)


def unit_rows(matrix):
    return matrix * lax.rsqrt(lax.optimization_barrier(jnp.sum(matrix * matrix, axis=-1, keepdims=True)) + 1e-06)

def reference(queries, key_heads, values_in, out_gate, log_decay, write_rate, cache_states, norm_gain, out_proj, hit_owner, hit_node, prefix_len, write_slot):
    head_group = VALUE_HEAD_HALF // HK
    group_width = VALUE_HEAD_HALF * DV // N_TENSOR

    def one_request(inputs):
        query_row, key_row, value_row, gate_row, decay_row, rate_row, slot_index, cached = inputs
        query_unit = unit_rows(query_row.astype(jnp.float32).reshape(NEW_TOKENS, HK, DK)) * DK ** (-0.5)
        key_unit = unit_rows(key_row.astype(jnp.float32).reshape(NEW_TOKENS, HK, DK))
        query_unit = jnp.repeat(query_unit, head_group, axis=1)
        key_unit = jnp.repeat(key_unit, head_group, axis=1)
        value_heads = value_row.astype(jnp.float32).reshape(NEW_TOKENS, VALUE_HEAD_HALF, DV)
        start_state = lax.dynamic_index_in_dim(cache_states, slot_index, 0, keepdims=False)
        start_state = jnp.where(cached > 0, start_state, jnp.zeros_like(start_state))

        def advance(running_state, token_row):
            query_at_step, key_at_step, value_t, decay_t, rate_t = token_row
            faded_state = running_state * jnp.exp(decay_t)[:, None, None]
            state_guess = jnp.einsum('qe,qep->qp', key_at_step, faded_state, precision=lax.Precision.HIGHEST)
            running_state = faded_state + (rate_t[:, None] * key_at_step)[:, :, None] * (value_t - state_guess)[:, None, :]
            state_readout = jnp.einsum('qe,qep->qp', query_at_step, running_state, precision=lax.Precision.HIGHEST)
            return (running_state, state_readout)
        final_state, attended = lax.scan(advance, start_state, (query_unit, key_unit, value_heads, decay_row.T, rate_row.T))
        gate_heads = gate_row.astype(jnp.float32).reshape(NEW_TOKENS, VALUE_HEAD_HALF, DV)
        scale_rows = lax.rsqrt(lax.optimization_barrier(jnp.mean(attended * attended, axis=-1, keepdims=True)) + 1e-06)
        normed = (attended * scale_rows * norm_gain * jax.nn.silu(gate_heads)).reshape(NEW_TOKENS, VALUE_HEAD_HALF * DV).astype(jnp.bfloat16)
        column_parts = normed.astype(jnp.float32).reshape(NEW_TOKENS, N_TENSOR, group_width)
        weight_parts = out_proj.astype(jnp.float32).reshape(N_TENSOR, group_width, D)
        partial_value = jnp.einsum('cgf,gfd->gcd', column_parts, weight_parts, precision=lax.Precision.HIGHEST).astype(jnp.bfloat16)
        partial_value = lax.optimization_barrier(partial_value).astype(jnp.float32)
        mixed = lax.optimization_barrier(jnp.sum(partial_value, axis=0)).astype(jnp.bfloat16)
        return (mixed, final_state)
    slot_ids = (hit_owner * CACHE_DEV + hit_node).astype(jnp.int32)
    mixed, finals = lax.map(one_request, (queries, key_heads, values_in, out_gate, log_decay, write_rate, slot_ids, prefix_len))
    end_states = jnp.zeros((REQUEST_TOTAL, VALUE_HEAD_HALF, DK, DV), jnp.float32).at[write_slot].set(finals)
    return (mixed, end_states)
```

```python
import jax
import jax.numpy as jnp
from jax import lax
from jax.experimental import pallas as pl
from jax.experimental.pallas import tpu as pltpu
from jax.sharding import PartitionSpec as P

DK = 128
DV = 128
REACH = 2
SMALL = 8

def split(x):
    hi = x.astype(jnp.bfloat16)
    return hi, (x - hi.astype(jnp.float32)).astype(jnp.bfloat16)


def dot1(a, b):
    return jnp.dot(a, b, preferred_element_type=jnp.float32)


def dot3(a, b):
    (a_hi, a_lo), (b_hi, b_lo) = a, b
    return dot1(a_hi, b_hi) + (dot1(a_lo, b_hi) + dot1(a_hi, b_lo))


def dot_nt(a, b):
    return lax.dot_general(a, b, (((1,), (1,)), ((), ())), preferred_element_type=jnp.float32)


def dot_tn(a, b):
    return lax.dot_general(a, b, (((0,), (0,)), ((), ())), preferred_element_type=jnp.float32)


def iota(shape, dim):
    return lax.broadcasted_iota(jnp.int32, shape, dim)


def solve_small(compact):
    rows, lanes = compact.shape
    place = iota((rows, lanes), 1) % SMALL
    inverse = jnp.where(place == iota((rows, lanes), 0) % SMALL, 1.0, 0.0)
    for j in range(SMALL - 1):
        column = jnp.where(place == j, compact, 0.0)
        if j:
            column = pltpu.roll(column, lanes - j, 1)
        for step in (1, 2, 4):
            column = column + pltpu.roll(column, step, 1)
        groups = inverse.reshape(rows // SMALL, SMALL, lanes)
        row = jnp.broadcast_to(groups[:, j : j + 1, :], groups.shape).reshape(rows, lanes)
        inverse = inverse - column * row
    return inverse


def invert_unit_lower(systems):
    n = systems[0].shape[0]
    half = n // 2
    block_of_lane = iota((n // SMALL, SMALL, n), 2) // SMALL
    own = block_of_lane == iota((n // SMALL, SMALL, n), 0)
    parts = []
    for system in systems:
        compact = jnp.sum(
            jnp.where(own, system.reshape(n // SMALL, SMALL, n), 0.0), axis=0
        )
        parts += [compact[:, :half], compact[:, half:]]
    small = solve_small(jnp.concatenate(parts, axis=0))
    inverses = []
    for i in range(len(systems)):
        left = small[2 * i * SMALL : (2 * i + 1) * SMALL]
        right = small[(2 * i + 1) * SMALL : (2 * i + 2) * SMALL]
        wide = jnp.concatenate([left, right], axis=1)
        inverses.append(
            jnp.where(own, jnp.broadcast_to(wide[None], own.shape), 0.0).reshape(n, n)
        )
    size = SMALL
    while size < half:
        pairs = n // (2 * size)
        even = iota((pairs, size, n), 2) // size == 2 * iota((pairs, size, n), 0)
        grown = []
        for system, inverse in zip(systems, inverses):
            below = jnp.where(even, system.reshape(pairs, 2, size, n)[:, 1], 0.0)
            folded = inverse.reshape(pairs, 2, size, n)
            lower = folded[:, 1].reshape(half, n)
            inner = dot3(split(below.reshape(half, n)), split(inverse))
            spread = jnp.stack(
                [jnp.zeros((pairs, size, n), jnp.float32), inner.reshape(pairs, size, n)], axis=1
            ).reshape(n, n)
            lower = lower - dot3(split(lower), split(spread))
            grown.append(
                jnp.stack([folded[:, 0], lower.reshape(pairs, size, n)], axis=1).reshape(n, n)
            )
        inverses = grown
        size *= 2
    done = []
    for system, inverse in zip(systems, inverses):
        top, bottom = inverse[:half, :half], inverse[half:, half:]
        cross = dot3(split(system[half:, :half]), split(top))
        cross = -dot3(split(bottom), split(cross))
        done.append(
            jnp.concatenate(
                [
                    jnp.concatenate([top, jnp.zeros_like(top)], axis=1),
                    jnp.concatenate([cross, bottom], axis=1),
                ],
                axis=0,
            )
        )
    return done


def prepare(r, q_ref, k_ref, v_ref, gate_ref, decay_ref, rate_ref, gain_ref, zhi_ref, zlo_ref, base_ref, gain_gate_ref):
    tokens = q_ref.shape[1]
    heads = decay_ref.shape[1]
    q, k = q_ref[r], k_ref[r]
    qf, kf = q.astype(jnp.float32), k.astype(jnp.float32)
    rq = lax.rsqrt(jnp.sum(qf * qf, axis=1, keepdims=True) + 1e-06) * DK ** (-0.5)
    k_square = jnp.sum(kf * kf, axis=1, keepdims=True)
    rk = lax.rsqrt(k_square + 1e-06)
    row, lane = iota((tokens, tokens), 0), iota((tokens, tokens), 1)
    raw_kk = dot_nt(k, k)
    raw_qk = dot_nt(q, k)
    rk_lane = lax.rsqrt(jnp.sum(jnp.where(row == lane, raw_kk, 0.0), axis=0, keepdims=True) + 1e-06)
    decay = decay_ref[r]
    hi, rest = split(decay)
    rest = decay - hi.astype(jnp.float32)
    mid, low = split(rest)
    upto = jnp.where(row <= lane, 1.0, 0.0).astype(jnp.bfloat16)
    running = dot1(low, upto) + dot1(mid, upto) + dot1(hi, upto)
    columns = jnp.concatenate(
        [running, rate_ref[r], jnp.zeros((8 - 2 * heads, tokens), jnp.float32)], axis=0
    ).T
    systems, reads = [], []
    for h in range(heads):
        spread = jnp.where(row >= lane, columns[:, h : h + 1] - running[h : h + 1], -jnp.inf)
        within = jnp.exp(spread) * rk_lane
        rate = columns[:, heads + h : heads + h + 1]
        systems.append(jnp.where(row > lane, (rate * rk) * (within * raw_kk), 0.0))
        reads.append(rq * (within * raw_qk))
    inverses = invert_unit_lower(systems)
    for h in range(heads):
        slot = r * heads + h
        g = columns[:, h : h + 1]
        rate = columns[:, heads + h : heads + h + 1]
        from_start = jnp.exp(g)
        values = v_ref[r, :, h * DV : (h + 1) * DV].astype(jnp.float32)
        right = jnp.concatenate([rate * values, (rate * from_start * rk) * kf], axis=1)
        solved = split(dot3(split(inverses[h]), split(right)))
        last = columns[tokens - 1 : tokens, h : h + 1]
        to_end = (jnp.exp(last - g) * rk) * kf
        read = dot3(split(reads[h]), solved)
        end_hi, end_lo = split(to_end)
        end = dot_tn(end_hi, solved[0]) + (dot_tn(end_lo, solved[0]) + dot_tn(end_hi, solved[1]))
        base_ref[slot, :tokens] = read[:, :DV]
        base_ref[slot, tokens:] = end[:, :DV]
        from_state = (from_start * rq) * qf - read[:, DV:]
        eye = iota((DK, DK), 0) == iota((DK, DK), 1)
        to_state = jnp.where(eye, jnp.exp(last), 0.0) - end[:, DV:]
        z_hi, z_lo = split(jnp.concatenate([from_state, to_state], axis=0))
        zhi_ref[slot] = z_hi
        zlo_ref[slot] = z_lo
        gate = gate_ref[r, :, h * DV : (h + 1) * DV].astype(jnp.float32)
        gain_gate_ref[slot] = gain_ref[...] * (gate / (1.0 + jnp.exp(-gate)))


def finish(slot, start, zhi_ref, zlo_ref, base_ref, gain_gate_ref):
    tokens = gain_gate_ref.shape[1]
    whole = dot1(zhi_ref[slot], start) + dot1(zlo_ref[slot], start) + base_ref[slot]
    attended, end = whole[:tokens], whole[tokens:]
    scale = lax.rsqrt(jnp.mean(attended * attended, axis=1, keepdims=True) + 1e-06)
    return (attended * scale * gain_gate_ref[slot]).astype(jnp.bfloat16), end


def delta_kernel(q_ref, k_ref, v_ref, gate_ref, decay_ref, rate_ref, gain_ref, start_ref, normed_ref, end_ref, zhi_ref, zlo_ref, base_ref, gain_gate_ref):
    heads = decay_ref.shape[1]

    @pl.loop(0, q_ref.shape[0])
    def _(r):
        prepare(r, q_ref, k_ref, v_ref, gate_ref, decay_ref, rate_ref, gain_ref, zhi_ref, zlo_ref, base_ref, gain_gate_ref)

    @pl.loop(0, q_ref.shape[0])
    def _(r):
        for h in range(heads):
            normed, end = finish(
                r * heads + h, start_ref[r, h].astype(jnp.bfloat16), zhi_ref, zlo_ref, base_ref, gain_gate_ref
            )
            normed_ref[r, :, h * DV : (h + 1) * DV] = normed
            end_ref[r, h] = end


def delta(q, k, v, gate, decay, rate, gain, start):
    requests, tokens = q.shape[:2]
    heads = decay.shape[1]
    return pl.pallas_call(
        delta_kernel,
        out_shape=(
            jax.ShapeDtypeStruct(v.shape, jnp.bfloat16),
            jax.ShapeDtypeStruct(start.shape, jnp.float32),
        ),
        scratch_shapes=[
            pltpu.VMEM((requests * heads, tokens + DK, DK), jnp.bfloat16),
            pltpu.VMEM((requests * heads, tokens + DK, DK), jnp.bfloat16),
            pltpu.VMEM((requests * heads, tokens + DK, DV), jnp.float32),
            pltpu.VMEM((requests * heads, tokens, DV), jnp.float32),
        ],
        compiler_params=pltpu.CompilerParams(vmem_limit_bytes=48 * 1024 * 1024),
        name="delta",
    )(q, k, v, gate, decay, rate, gain, start)


def shifted(x, axis, by):
    devices = lax.axis_size(axis)
    return lax.ppermute(x, axis, [(i, (i + by) % devices) for i in range(devices)])


def on_device(
    queries,
    key_heads,
    values_in,
    out_gate,
    log_decay,
    write_rate,
    cache_states,
    norm_gain,
    out_proj,
    hit_owner,
    hit_node,
    prefix_len,
    write_slot,
):
    requests_here, length = queries.shape[:2]
    head_count = log_decay.shape[1]
    slot_count = cache_states.shape[0]
    workers = lax.axis_size("worker")
    worker_id = lax.axis_index("worker")
    cached = prefix_len > 0
    relative = (hit_owner - worker_id + workers + REACH) % workers - REACH
    pieces = []
    for offset in range(-REACH, REACH + 1):
        if offset == 0:
            pieces.append(cache_states)
        else:
            pieces.append(shifted(cache_states, "worker", -offset))
    window = jnp.concatenate(pieces, axis=0)
    start_state = jnp.take(window, (relative + REACH) * slot_count + hit_node, axis=0)
    start_state = jnp.where(cached[:, None, None, None], start_state, 0.0)
    normed, running_state = delta(
        queries, key_heads, values_in, out_gate, log_decay, write_rate, norm_gain[None], start_state
    )
    partial_value = jnp.dot(
        normed.reshape(requests_here * length, head_count * DV), out_proj, preferred_element_type=jnp.float32
    ).reshape(requests_here, length, out_proj.shape[1])
    mixed = lax.psum_scatter(
        partial_value.astype(jnp.bfloat16), "tensor", scatter_dimension=2, tiled=True
    )
    target_worker = write_slot // requests_here
    target_lane = write_slot % requests_here
    target_move = (target_worker - worker_id + workers + REACH) % workers - REACH
    lane_ids = jnp.arange(requests_here, dtype=jnp.int32)
    end_states = jnp.zeros_like(running_state)
    for offset in range(-REACH, REACH + 1):
        routed = (target_move == offset)[:, None] & (target_lane[:, None] == lane_ids[None, :])
        packed = jnp.sum(
            jnp.where(routed[:, :, None, None, None], running_state[:, None], 0.0), axis=0
        )
        if offset != 0:
            packed = shifted(packed.astype(jnp.bfloat16), "worker", offset).astype(packed.dtype)
        end_states = end_states + packed
    return (mixed, end_states)


def solution(mesh):
    in_specs = (
        P("worker", None, "tensor"),
        P("worker", None, "tensor"),
        P("worker", None, "tensor"),
        P("worker", None, "tensor"),
        P("worker", "tensor", None),
        P("worker", "tensor", None),
        P("worker", "tensor", None, None),
        P(),
        P("tensor", None),
        P("worker"),
        P("worker"),
        P("worker"),
        P("worker"),
    )
    out_specs = (P("worker", None, "tensor"), P("worker", "tensor", None, None))
    return jax.shard_map(
        on_device, mesh=mesh, in_specs=in_specs, out_specs=out_specs, check_vma=False
    )
```

```python
import functools

import jax
import jax.numpy as jnp
from jax import lax
from jax.experimental import pallas as pl
from jax.experimental.pallas import tpu as pltpu
from jax.sharding import PartitionSpec as P

DK = 128
DV = 128
REACH = 2
SMALL = 8
MESH = pl.DeviceIdType.MESH
OFFSETS = (-2, 2, -1, 1)
CORE, PAIR, CROSS, FAR = range(4)


def split(x):
    hi = x.astype(jnp.bfloat16)
    return hi, (x - hi.astype(jnp.float32)).astype(jnp.bfloat16)


def dot1(a, b):
    return jnp.dot(a, b, preferred_element_type=jnp.float32)


def dot3(a, b):
    (a_hi, a_lo), (b_hi, b_lo) = a, b
    return dot1(a_hi, b_hi) + (dot1(a_lo, b_hi) + dot1(a_hi, b_lo))


def dot_nt(a, b):
    return lax.dot_general(a, b, (((1,), (1,)), ((), ())), preferred_element_type=jnp.float32)


def dot_tn(a, b):
    return lax.dot_general(a, b, (((0,), (0,)), ((), ())), preferred_element_type=jnp.float32)


def iota(shape, dim):
    return lax.broadcasted_iota(jnp.int32, shape, dim)


def solve_small(compact):
    rows, lanes = compact.shape
    place = iota((rows, lanes), 1) % SMALL
    inverse = jnp.where(place == iota((rows, lanes), 0) % SMALL, 1.0, 0.0)
    for j in range(SMALL - 1):
        column = jnp.where(place == j, compact, 0.0)
        if j:
            column = pltpu.roll(column, lanes - j, 1)
        for step in (1, 2, 4):
            column = column + pltpu.roll(column, step, 1)
        groups = inverse.reshape(rows // SMALL, SMALL, lanes)
        row = jnp.broadcast_to(groups[:, j : j + 1, :], groups.shape).reshape(rows, lanes)
        inverse = inverse - column * row
    return inverse


def invert_unit_lower(systems):
    n = systems[0].shape[0]
    half = n // 2
    block_of_lane = iota((n // SMALL, SMALL, n), 2) // SMALL
    own = block_of_lane == iota((n // SMALL, SMALL, n), 0)
    parts = []
    for system in systems:
        compact = jnp.sum(
            jnp.where(own, system.reshape(n // SMALL, SMALL, n), 0.0), axis=0
        )
        parts += [compact[:, :half], compact[:, half:]]
    small = solve_small(jnp.concatenate(parts, axis=0))
    inverses = []
    for i in range(len(systems)):
        left = small[2 * i * SMALL : (2 * i + 1) * SMALL]
        right = small[(2 * i + 1) * SMALL : (2 * i + 2) * SMALL]
        wide = jnp.concatenate([left, right], axis=1)
        inverses.append(
            jnp.where(own, jnp.broadcast_to(wide[None], own.shape), 0.0).reshape(n, n)
        )
    size = SMALL
    while size < half:
        pairs = n // (2 * size)
        even = iota((pairs, size, n), 2) // size == 2 * iota((pairs, size, n), 0)
        grown = []
        for system, inverse in zip(systems, inverses):
            below = jnp.where(even, system.reshape(pairs, 2, size, n)[:, 1], 0.0)
            folded = inverse.reshape(pairs, 2, size, n)
            lower = folded[:, 1].reshape(half, n)
            inner = dot3(split(below.reshape(half, n)), split(inverse))
            spread = jnp.stack(
                [jnp.zeros((pairs, size, n), jnp.float32), inner.reshape(pairs, size, n)], axis=1
            ).reshape(n, n)
            lower = lower - dot3(split(lower), split(spread))
            grown.append(
                jnp.stack([folded[:, 0], lower.reshape(pairs, size, n)], axis=1).reshape(n, n)
            )
        inverses = grown
        size *= 2
    done = []
    for system, inverse in zip(systems, inverses):
        top, bottom = inverse[:half, :half], inverse[half:, half:]
        cross = dot3(split(system[half:, :half]), split(top))
        cross = -dot3(split(bottom), split(cross))
        done.append(
            jnp.concatenate(
                [
                    jnp.concatenate([top, jnp.zeros_like(top)], axis=1),
                    jnp.concatenate([cross, bottom], axis=1),
                ],
                axis=0,
            )
        )
    return done


def prepare(r, q_ref, k_ref, v_ref, gate_ref, decay_ref, rate_ref, gain_ref, zhi_ref, zlo_ref, base_ref, gain_gate_ref):
    tokens = q_ref.shape[1]
    heads = decay_ref.shape[1]
    q, k = q_ref[r], k_ref[r]
    qf, kf = q.astype(jnp.float32), k.astype(jnp.float32)
    rq = lax.rsqrt(jnp.sum(qf * qf, axis=1, keepdims=True) + 1e-06) * DK ** (-0.5)
    k_square = jnp.sum(kf * kf, axis=1, keepdims=True)
    rk = lax.rsqrt(k_square + 1e-06)
    row, lane = iota((tokens, tokens), 0), iota((tokens, tokens), 1)
    raw_kk = dot_nt(k, k)
    raw_qk = dot_nt(q, k)
    rk_lane = lax.rsqrt(jnp.sum(jnp.where(row == lane, raw_kk, 0.0), axis=0, keepdims=True) + 1e-06)
    decay = decay_ref[r]
    hi, rest = split(decay)
    rest = decay - hi.astype(jnp.float32)
    mid, low = split(rest)
    upto = jnp.where(row <= lane, 1.0, 0.0).astype(jnp.bfloat16)
    running = dot1(low, upto) + dot1(mid, upto) + dot1(hi, upto)
    columns = jnp.concatenate(
        [running, rate_ref[r], jnp.zeros((8 - 2 * heads, tokens), jnp.float32)], axis=0
    ).T
    systems, reads = [], []
    for h in range(heads):
        spread = jnp.where(row >= lane, columns[:, h : h + 1] - running[h : h + 1], -jnp.inf)
        within = jnp.exp(spread) * rk_lane
        rate = columns[:, heads + h : heads + h + 1]
        systems.append(jnp.where(row > lane, (rate * rk) * (within * raw_kk), 0.0))
        reads.append(rq * (within * raw_qk))
    inverses = invert_unit_lower(systems)
    for h in range(heads):
        slot = r * heads + h
        g = columns[:, h : h + 1]
        rate = columns[:, heads + h : heads + h + 1]
        from_start = jnp.exp(g)
        values = v_ref[r, :, h * DV : (h + 1) * DV].astype(jnp.float32)
        right = jnp.concatenate([rate * values, (rate * from_start * rk) * kf], axis=1)
        solved = split(dot3(split(inverses[h]), split(right)))
        last = columns[tokens - 1 : tokens, h : h + 1]
        to_end = (jnp.exp(last - g) * rk) * kf
        read = dot3(split(reads[h]), solved)
        end_hi, end_lo = split(to_end)
        end = dot_tn(end_hi, solved[0]) + (dot_tn(end_lo, solved[0]) + dot_tn(end_hi, solved[1]))
        base_ref[slot, :tokens] = read[:, :DV]
        base_ref[slot, tokens:] = end[:, :DV]
        from_state = (from_start * rq) * qf - read[:, DV:]
        eye = iota((DK, DK), 0) == iota((DK, DK), 1)
        to_state = jnp.where(eye, jnp.exp(last), 0.0) - end[:, DV:]
        z_hi, z_lo = split(jnp.concatenate([from_state, to_state], axis=0))
        zhi_ref[slot] = z_hi
        zlo_ref[slot] = z_lo
        gate = gate_ref[r, :, h * DV : (h + 1) * DV].astype(jnp.float32)
        gain_gate_ref[slot] = gain_ref[...] * (gate / (1.0 + jnp.exp(-gate)))


def finish(slot, start, zhi_ref, zlo_ref, base_ref, gain_gate_ref):
    tokens = gain_gate_ref.shape[1]
    whole = dot1(zhi_ref[slot], start) + dot1(zlo_ref[slot], start) + base_ref[slot]
    attended, end = whole[:tokens], whole[tokens:]
    scale = lax.rsqrt(jnp.mean(attended * attended, axis=1, keepdims=True) + 1e-06)
    return (attended * scale * gain_gate_ref[slot]).astype(jnp.bfloat16), end


def layer_kernel(
    workers,
    owner_ref,
    node_ref,
    prefix_ref,
    slot_ref,
    gain_ref,
    q_hbm,
    k_hbm,
    v_hbm,
    gate_hbm,
    decay_hbm,
    rate_hbm,
    cache_hbm,
    proj_hbm,
    mixed_ref,
    end_ref,
    q_ref,
    k_ref,
    v_ref,
    gate_ref,
    decay_ref,
    rate_ref,
    cache_ref,
    zhi_ref,
    zlo_ref,
    base_ref,
    gain_gate_ref,
    info_ref,
    told_ref,
    told_smem,
    lent_ref,
    borrowed_ref,
    own_end_ref,
    sent_end_ref,
    got_end_ref,
    weight_ref,
    normed_ref,
    kept_ref,
    passed_ref,
    got_ref,
    load_sem,
    weight_load_sem,
    told_sem,
    info_send,
    info_recv,
    lend_send,
    lend_recv,
    end_send,
    end_recv,
    weight_send,
    weight_recv,
    normed_send,
    normed_recv,
    partial_send,
    partial_recv,
):
    requests, tokens = q_ref.shape[:2]
    heads = decay_ref.shape[1]
    width = heads * DV
    slots = cache_ref.shape[0]
    worker = lax.axis_index("worker")
    tensor = lax.axis_index("tensor")
    chip, core = tensor // 2, tensor % 2
    pair_chip = chip + 1 - 2 * (chip % 2)
    far_chip = 3 - chip
    near = [(lax.rem(worker + workers + o, workers), tensor) for o in OFFSETS]
    side = [
        (worker, 2 * chip + 1 - core),
        (worker, 2 * pair_chip + core),
        (worker, 2 * pair_chip + 1 - core),
        (worker, 2 * far_chip + core),
    ]

    def remote(src, dst, send, recv, device):
        return pltpu.make_async_remote_copy(
            src_ref=src, dst_ref=dst, send_sem=send, recv_sem=recv, device_id=device, device_id_type=MESH
        )

    loads = [
        pltpu.make_async_copy(src, dst, load_sem.at[i])
        for i, (src, dst) in enumerate(
            (
                (q_hbm, q_ref),
                (k_hbm, k_ref),
                (v_hbm, v_ref),
                (decay_hbm, decay_ref),
                (rate_hbm, rate_ref),
                (gate_hbm, gate_ref),
                (cache_hbm, cache_ref),
            )
        )
    ]
    for load in loads:
        load.start()

    def columns(index):
        return pl.ds(pl.multiple_of(index * width, width), width)

    def far_of(index):
        return 2 * (3 - index // 2) + index % 2

    weight_loads = [
        pltpu.make_async_copy(
            proj_hbm.at[:, columns(index)], weight_ref.at[0, :, pl.ds(part * width, width)], weight_load_sem.at[part]
        )
        for part, index in enumerate((tensor, far_of(tensor)))
    ]
    for load in weight_loads:
        load.start()

    lane = iota((8, 128), 1)
    block = jnp.zeros((8, 128), jnp.int32)
    for part, ref in enumerate((owner_ref, node_ref, prefix_ref, slot_ref)):
        for i in range(requests):
            block = jnp.where(lane == part * requests + i, ref[i], block)
    info_ref[...] = block

    barrier = pltpu.get_barrier_semaphore()
    for device in near + side:
        pl.semaphore_signal(barrier, inc=1, device_id=device, device_id_type=MESH)
    pl.semaphore_wait(barrier, len(near) + len(side))

    def opposite(n):
        return n ^ 1

    infos = [
        remote(info_ref, told_ref.at[opposite(n)], info_send.at[n], info_recv.at[opposite(n)], near[n])
        for n in range(4)
    ]
    for copy in infos:
        copy.start()

    weights = []
    for kind in (CORE, PAIR, CROSS):
        index = side[kind][1]
        for part, target in enumerate((index, far_of(index))):
            n = 2 * kind + part
            weights.append(
                remote(
                    proj_hbm.at[:, columns(target)],
                    weight_ref.at[kind + 1, :, pl.ds(part * width, width)],
                    weight_send.at[n],
                    weight_recv.at[n],
                    side[kind],
                )
            )
    for copy in weights:
        copy.start()

    def lend(n, i):
        return remote(
            lent_ref.at[n, i], borrowed_ref.at[opposite(n), i], lend_send.at[n, i], lend_recv.at[opposite(n), i], near[n]
        )

    def borrow(n, i):
        return remote(
            lent_ref.at[n, i], borrowed_ref.at[n, i], lend_send.at[n, i], lend_recv.at[n, i], near[n]
        )

    def send_end(n, i):
        return remote(
            sent_end_ref.at[i], got_end_ref.at[opposite(n), i], end_send.at[n, i], end_recv.at[opposite(n), i], near[n]
        )

    def get_end(n, i):
        return remote(sent_end_ref.at[i], got_end_ref.at[n, i], end_send.at[n, i], end_recv.at[n, i], near[n])

    def send_normed(kind, i):
        source = 2 if kind == CROSS else 0
        device = side[PAIR] if kind == PAIR else side[CORE]
        return remote(
            normed_ref.at[i, source],
            normed_ref.at[i, kind + 1],
            normed_send.at[kind, i],
            normed_recv.at[kind, i],
            device,
        )

    def send_partial(i):
        return remote(passed_ref.at[i], got_ref.at[i], partial_send.at[i], partial_recv.at[i], side[FAR])

    def answer():
        for n in range(4):
            remote(info_ref, told_ref.at[n], info_send.at[n], info_recv.at[n], near[n]).wait_recv()
        fetch = pltpu.make_async_copy(told_ref, told_smem, told_sem)
        fetch.start()
        fetch.wait()
        loads[6].wait()
        for i in range(requests):
            for n in range(4):
                node = jnp.clip(told_smem[n, 0, requests + i], 0, slots - 1)
                lent_ref[n, i] = cache_ref[node].astype(jnp.bfloat16)
                lend(n, i).start()

    def complete(i):
        for n in range(4):
            borrow(n, i).wait_recv()
        move = lax.rem(owner_ref[i] - worker + workers + REACH, workers) - REACH
        node = jnp.clip(node_ref[i], 0, slots - 1)
        cached = prefix_ref[i] > 0
        for h in range(heads):
            start = cache_ref[node, h].astype(jnp.bfloat16)
            for n, offset in enumerate(OFFSETS):
                start = jnp.where(move == offset, borrowed_ref[n, i, h], start)
            start = jnp.where(cached, start, jnp.zeros_like(start))
            normed, end = finish(i * heads + h, start, zhi_ref, zlo_ref, base_ref, gain_gate_ref)
            normed_ref[i, 0, :, h * DV : (h + 1) * DV] = normed
            own_end_ref[i, h] = end
            sent_end_ref[i, h] = end.astype(jnp.bfloat16)
        send_normed(PAIR, i).start()
        send_normed(CORE, i).start()
        for n in range(4):
            send_end(n, i).start()

    def forward(i):
        send_normed(PAIR, i).wait_recv()
        send_normed(CROSS, i).start()

    def project(i):
        send_normed(CORE, i).wait_recv()
        send_normed(CROSS, i).wait_recv()
        total = dot1(normed_ref[i, 0], weight_ref[0])
        for source in range(1, 4):
            total = total + dot1(normed_ref[i, source], weight_ref[source])
        kept_ref[i] = total[:, :width]
        passed_ref[i] = total[:, width:].astype(jnp.bfloat16)
        send_partial(i).start()

    def add(i):
        send_partial(i).wait_recv()
        mixed_ref[i] = (kept_ref[i] + got_ref[i].astype(jnp.float32)).astype(jnp.bfloat16)

    for load in loads[:6]:
        load.wait()

    @pl.loop(0, requests + 4)
    def _(step):
        @pl.when(step < requests)
        def _():
            prepare(
                step, q_ref, k_ref, v_ref, gate_ref, decay_ref, rate_ref, gain_ref, zhi_ref, zlo_ref, base_ref, gain_gate_ref
            )

        @pl.when(step == 0)
        def _():
            answer()

        @pl.when((step >= 1) & (step < requests + 1))
        def _():
            complete(step - 1)

        @pl.when((step >= 2) & (step < requests + 2))
        def _():
            forward(step - 2)

        @pl.when(step == 3)
        def _():
            for load in weight_loads:
                load.wait()
            for copy in weights:
                copy.wait_recv()

        @pl.when((step >= 3) & (step < requests + 3))
        def _():
            project(step - 3)

        @pl.when(step >= 4)
        def _():
            add(step - 4)

    for i in range(requests):
        for n in range(4):
            get_end(n, i).wait_recv()
    for target in range(requests):
        row = worker * requests + target
        mine, theirs = jnp.int32(0), jnp.int32(0)
        kept = jnp.bool_(False)
        for i in range(requests):
            here = slot_ref[i] == row
            kept = kept | here
            mine = jnp.where(here, i, mine)
            for n in range(4):
                theirs = jnp.where(told_smem[n, 0, 3 * requests + i] == row, n * requests + i, theirs)
        for h in range(heads):
            end_ref[target, h] = jnp.where(
                kept, own_end_ref[mine, h], got_end_ref[theirs // requests, theirs % requests, h].astype(jnp.float32)
            )

    for copy in infos + weights:
        copy.wait_send()
    for i in range(requests):
        for n in range(4):
            lend(n, i).wait_send()
            send_end(n, i).wait_send()
        for kind in (CORE, PAIR, CROSS):
            send_normed(kind, i).wait_send()
        send_partial(i).wait_send()


def on_device(
    queries,
    key_heads,
    values_in,
    out_gate,
    log_decay,
    write_rate,
    cache_states,
    norm_gain,
    out_proj,
    hit_owner,
    hit_node,
    prefix_len,
    write_slot,
):
    requests, tokens = queries.shape[:2]
    heads = log_decay.shape[1]
    width = heads * DV
    state = cache_states.shape[1:]
    smem = pl.BlockSpec(memory_space=pltpu.SMEM)
    vmem = pl.BlockSpec(memory_space=pltpu.VMEM)
    anywhere = pl.BlockSpec(memory_space=pltpu.HBM)
    low, wide = jnp.bfloat16, jnp.float32
    dma = pltpu.SemaphoreType.DMA
    return pl.pallas_call(
        functools.partial(layer_kernel, lax.axis_size("worker")),
        out_shape=(
            jax.ShapeDtypeStruct((requests, tokens, width), low),
            jax.ShapeDtypeStruct((requests, *state), wide),
        ),
        in_specs=[smem] * 4 + [vmem] + [anywhere] * 8,
        out_specs=(vmem, vmem),
        scratch_shapes=[
            pltpu.VMEM(queries.shape, low),
            pltpu.VMEM(key_heads.shape, low),
            pltpu.VMEM(values_in.shape, low),
            pltpu.VMEM(out_gate.shape, low),
            pltpu.VMEM(log_decay.shape, wide),
            pltpu.VMEM(write_rate.shape, wide),
            pltpu.VMEM(cache_states.shape, wide),
            pltpu.VMEM((requests * heads, tokens + DK, DK), low),
            pltpu.VMEM((requests * heads, tokens + DK, DK), low),
            pltpu.VMEM((requests * heads, tokens + DK, DV), wide),
            pltpu.VMEM((requests * heads, tokens, DV), wide),
            pltpu.VMEM((8, 128), jnp.int32),
            pltpu.VMEM((4, 8, 128), jnp.int32),
            pltpu.SMEM((4, 8, 128), jnp.int32),
            pltpu.VMEM((4, requests, *state), low),
            pltpu.VMEM((4, requests, *state), low),
            pltpu.VMEM((requests, *state), wide),
            pltpu.VMEM((requests, *state), low),
            pltpu.VMEM((4, requests, *state), low),
            pltpu.VMEM((4, width, 2 * width), low),
            pltpu.VMEM((requests, 4, tokens, width), low),
            pltpu.VMEM((requests, tokens, width), wide),
            pltpu.VMEM((requests, tokens, width), low),
            pltpu.VMEM((requests, tokens, width), low),
            dma((7,)),
            dma((2,)),
            dma,
            dma((4,)),
            dma((4,)),
            dma((4, requests)),
            dma((4, requests)),
            dma((4, requests)),
            dma((4, requests)),
            dma((6,)),
            dma((6,)),
            dma((3, requests)),
            dma((3, requests)),
            dma((requests,)),
            dma((requests,)),
        ],
        compiler_params=pltpu.CompilerParams(
            collective_id=0, has_side_effects=True, vmem_limit_bytes=60 * 1024 * 1024
        ),
        name="layer",
    )(
        hit_owner,
        hit_node,
        prefix_len,
        write_slot,
        norm_gain[None],
        queries,
        key_heads,
        values_in,
        out_gate,
        log_decay,
        write_rate,
        cache_states,
        out_proj,
    )


def solution(mesh):
    in_specs = (
        P("worker", None, "tensor"),
        P("worker", None, "tensor"),
        P("worker", None, "tensor"),
        P("worker", None, "tensor"),
        P("worker", "tensor", None),
        P("worker", "tensor", None),
        P("worker", "tensor", None, None),
        P(),
        P("tensor", None),
        P("worker"),
        P("worker"),
        P("worker"),
        P("worker"),
    )
    out_specs = (P("worker", None, "tensor"), P("worker", "tensor", None, None))
    return jax.shard_map(
        on_device, mesh=mesh, in_specs=in_specs, out_specs=out_specs, check_vma=False
    )
```

```python
import functools

import jax
import jax.numpy as jnp
from jax import lax
from jax.experimental import pallas as pl
from jax.experimental.pallas import tpu as pltpu
from jax.sharding import PartitionSpec as P

DK = 128
DV = 128
REACH = 2
SMALL = 8
MESH = pl.DeviceIdType.MESH
OFFSETS = (-2, 2, -1, 1)
TWIN, MATE, CROSS = range(3)


def split(x):
    hi = x.astype(jnp.bfloat16)
    return hi, (x - hi.astype(jnp.float32)).astype(jnp.bfloat16)


def dot1(a, b):
    return jnp.dot(a, b, preferred_element_type=jnp.float32)


def dot3(a, b):
    (a_hi, a_lo), (b_hi, b_lo) = a, b
    return dot1(jnp.concatenate([a_hi, a_lo, a_hi], axis=1), jnp.concatenate([b_hi, b_hi, b_lo], axis=0))


def dot_nt(a, b):
    return lax.dot_general(a, b, (((1,), (1,)), ((), ())), preferred_element_type=jnp.float32)


def dot_tn(a, b):
    return lax.dot_general(a, b, (((0,), (0,)), ((), ())), preferred_element_type=jnp.float32)


def iota(shape, dim):
    return lax.broadcasted_iota(jnp.int32, shape, dim)


def solve_small(compact):
    rows, lanes = compact.shape
    place = iota((rows, lanes), 1) % SMALL
    inverse = jnp.where(place == iota((rows, lanes), 0) % SMALL, 1.0, 0.0)
    for j in range(SMALL - 1):
        column = jnp.where(place == j, compact, 0.0)
        if j:
            column = pltpu.roll(column, lanes - j, 1)
        for step in (1, 2, 4):
            column = column + pltpu.roll(column, step, 1)
        groups = inverse.reshape(rows // SMALL, SMALL, lanes)
        row = jnp.broadcast_to(groups[:, j : j + 1, :], groups.shape).reshape(rows, lanes)
        inverse = inverse - column * row
    return inverse


def invert_unit_lower(systems):
    n = systems[0].shape[0]
    own = iota((n, n), 1) // SMALL == iota((n, n), 0) // SMALL
    compact = [
        jnp.sum(jnp.where(own, system, 0.0).reshape(n // SMALL, SMALL, n), axis=0) for system in systems
    ]
    small = solve_small(jnp.concatenate(compact, axis=0))
    inverses = []
    for i in range(len(systems)):
        block = small[i * SMALL : (i + 1) * SMALL]
        wide = jnp.broadcast_to(block[None], (n // SMALL, SMALL, n)).reshape(n, n)
        inverses.append(jnp.where(own, wide, 0.0))
    parts = [split(system) for system in systems]
    size = SMALL
    while size < n:
        row, lane = iota((n, n), 0) // size, iota((n, n), 1) // size
        below = (row % 2 == 1) & (row == lane + 1)
        cut = [tuple(jnp.where(below, part, jnp.zeros_like(part)) for part in pair) for pair in parts]
        halves = [split(inverse) for inverse in inverses]
        inner = [split(dot3(x, y)) for x, y in zip(cut, halves)]
        inverses = [inverse - dot3(x, y) for inverse, x, y in zip(inverses, halves, inner)]
        size *= 2
    return inverses


def prepare(
    rs, between, q_ref, k_ref, v_ref, gate_ref, decay_ref, rate_ref, gain_ref, zhi_ref, zlo_ref, base_ref, gain_gate_ref
):
    tokens = q_ref.shape[1]
    heads = decay_ref.shape[1]
    half = tokens // 2
    row, lane = iota((half, half), 0), iota((half, half), 1)
    upto = jnp.where(iota((tokens, tokens), 0) <= iota((tokens, tokens), 1), 1.0, 0.0).astype(jnp.bfloat16)
    decay = jnp.concatenate([decay_ref[r] for r in rs], axis=0)
    hi, _ = split(decay)
    rest = decay - hi.astype(jnp.float32)
    mid, low = split(rest)
    sums = dot1(jnp.concatenate([hi, mid, low], axis=0), upto)
    count = len(rs) * heads
    runnings = sums[2 * count :] + sums[count : 2 * count] + sums[:count]
    every = [runnings] + [rate_ref[r] for r in rs]
    pad = -2 * count % 8
    if pad:
        every.append(jnp.zeros((pad, tokens), jnp.float32))
    columns = jnp.concatenate(every, axis=0).T
    chains = []
    for n, r in enumerate(rs):
        q, k = q_ref[r], k_ref[r]
        qf, kf = q.astype(jnp.float32), k.astype(jnp.float32)
        rq = lax.rsqrt(jnp.sum(qf * qf, axis=1, keepdims=True) + 1e-06) * DK ** (-0.5)
        rk = lax.rsqrt(jnp.sum(kf * kf, axis=1, keepdims=True) + 1e-06)
        first, second = dot_nt(k, k[:half]), dot_nt(k[half:], k[half:])
        scales = [
            lax.rsqrt(jnp.sum(jnp.where(row == lane, raw, 0.0), axis=0, keepdims=True) + 1e-06)
            for raw in (first[:half], second)
        ]
        kk = [
            first[:half] * (scales[0] * rk[:half]),
            first[half:] * (scales[0] * rk[half:]),
            second * (scales[1] * rk[half:]),
        ]
        first, second = dot_nt(q, k[:half]), dot_nt(q[half:], k[half:])
        qk = [
            first[:half] * (scales[0] * rq[:half]),
            first[half:] * (scales[0] * rq[half:]),
            second * (scales[1] * rq[half:]),
        ]
        for h in range(heads):
            c = n * heads + h
            chains.append((r, h, qf, kf, rq, rk, kk, qk, columns[:, c : c + 1], columns[:, count + c : count + c + 1], runnings[c : c + 1]))
    systems, crosses, reads = [], [], []
    for r, h, qf, kf, rq, rk, kk, qk, g, rate, ahead in chains:
        within = [
            jnp.exp(jnp.where(row >= lane, g[:half] - ahead[:, :half], -jnp.inf)),
            jnp.exp(g[half:] - ahead[:, :half]),
            jnp.exp(jnp.where(row >= lane, g[half:] - ahead[:, half:], -jnp.inf)),
        ]
        systems.append(jnp.where(row > lane, rate[:half] * (within[0] * kk[0]), 0.0))
        systems.append(jnp.where(row > lane, rate[half:] * (within[2] * kk[2]), 0.0))
        crosses.append(split(rate[half:] * (within[1] * kk[1])))
        reads.append([split(x * y) for x, y in zip(within, qk)])
    inverses = [split(x) for x in invert_unit_lower(systems)]
    between()
    rights = []
    for r, h, qf, kf, rq, rk, kk, qk, g, rate, ahead in chains:
        values = v_ref[r, :, h * DV : (h + 1) * DV].astype(jnp.float32)
        rights.append(jnp.concatenate([rate * values, (rate * jnp.exp(g) * rk) * kf], axis=1))
    tops = [split(dot3(x, split(y[:half]))) for x, y in zip(inverses[::2], rights)]
    rests = [y[half:] - dot3(x, top) for x, y, top in zip(crosses, rights, tops)]
    bottoms = [split(dot3(x, split(rest))) for x, rest in zip(inverses[1::2], rests)]
    solveds = [
        tuple(jnp.concatenate([x, y], axis=0) for x, y in zip(top, bottom)) for top, bottom in zip(tops, bottoms)
    ]
    read_tops = [dot3(read[0], top) for read, top in zip(reads, tops)]
    read_bottoms = [
        dot3(tuple(jnp.concatenate([x, y], axis=1) for x, y in zip(read[1], read[2])), solved)
        for read, solved in zip(reads, solveds)
    ]
    ends = []
    for (r, h, qf, kf, rq, rk, kk, qk, g, rate, ahead), solved in zip(chains, solveds):
        hi, lo = split((jnp.exp(g[tokens - 1 :] - g) * rk) * kf)
        ends.append(dot_tn(jnp.concatenate([hi, lo, hi], axis=0), jnp.concatenate([solved[0], solved[0], solved[1]], axis=0)))
    eye = iota((DK, DK), 0) == iota((DK, DK), 1)
    for (r, h, qf, kf, rq, rk, kk, qk, g, rate, ahead), top, bottom, end in zip(chains, read_tops, read_bottoms, ends):
        slot = r * heads + h
        base_ref[slot, :half] = top[:, :DV]
        base_ref[slot, half:tokens] = bottom[:, :DV]
        base_ref[slot, tokens:] = end[:, :DV]
        from_state = (jnp.exp(g) * rq) * qf - jnp.concatenate([top[:, DV:], bottom[:, DV:]], axis=0)
        to_state = jnp.where(eye, jnp.exp(g[tokens - 1 :]), 0.0) - end[:, DV:]
        z_hi, z_lo = split(jnp.concatenate([from_state, to_state], axis=0))
        zhi_ref[slot] = z_hi
        zlo_ref[slot] = z_lo
        gate = gate_ref[r, :, h * DV : (h + 1) * DV].astype(jnp.float32)
        gain_gate_ref[slot] = gain_ref[...] * (gate / (1.0 + jnp.exp(-gate)))


def finish(slots, starts, zhi_ref, zlo_ref, base_ref, gain_gate_ref):
    tokens = gain_gate_ref.shape[1]
    wholes = [
        dot1(zhi_ref[slot], start) + dot1(zlo_ref[slot], start) + base_ref[slot] for slot, start in zip(slots, starts)
    ]
    scales = [
        lax.rsqrt(jnp.mean(whole[:tokens] * whole[:tokens], axis=1, keepdims=True) + 1e-06) for whole in wholes
    ]
    normed = [
        (whole[:tokens] * scale * gain_gate_ref[slot]).astype(jnp.bfloat16)
        for slot, whole, scale in zip(slots, wholes, scales)
    ]
    return normed, [whole[tokens:] for whole in wholes]


def layer_kernel(
    workers,
    owner_ref,
    node_ref,
    prefix_ref,
    slot_ref,
    gain_ref,
    q_hbm,
    k_hbm,
    v_hbm,
    gate_hbm,
    decay_hbm,
    rate_hbm,
    cache_hbm,
    proj_hbm,
    mixed_ref,
    end_ref,
    q_ref,
    k_ref,
    v_ref,
    gate_ref,
    decay_ref,
    rate_ref,
    cache_ref,
    zhi_ref,
    zlo_ref,
    base_ref,
    gain_gate_ref,
    info_ref,
    told_ref,
    told_smem,
    hop_out_ref,
    hop_in_ref,
    lent_ref,
    borrowed_ref,
    sent_end_ref,
    got_end_ref,
    weight_ref,
    normed_ref,
    kept_ref,
    passed_ref,
    got_ref,
    load_sem,
    weight_load_sem,
    told_sem,
    info_send,
    info_recv,
    hop_send,
    hop_recv,
    lend_send,
    lend_recv,
    end_send,
    end_recv,
    weight_send,
    weight_recv,
    normed_send,
    normed_recv,
    partial_send,
    partial_recv,
):
    requests, tokens = q_ref.shape[:2]
    heads = decay_ref.shape[1]
    width = heads * DV
    slots = cache_ref.shape[0]
    worker = lax.axis_index("worker")
    tensor = lax.axis_index("tensor")
    chip, core = tensor // 2, tensor % 2

    def paired(index, way):
        there = index // 2
        mate = 3 - there if way else there + 1 - 2 * (there % 2)
        return 2 * mate + index % 2

    near = [(lax.rem(worker + workers + o, workers), tensor) for o in OFFSETS]
    twin = 2 * chip + 1 - core
    sides = [(twin, paired(tensor, way), paired(twin, way)) for way in range(2)]
    others = [twin, *sides[0][1:], *sides[1][1:]]

    def remote(src, dst, send, recv, device):
        return pltpu.make_async_remote_copy(
            src_ref=src, dst_ref=dst, send_sem=send, recv_sem=recv, device_id=device, device_id_type=MESH
        )

    loads = [
        pltpu.make_async_copy(src, dst, load_sem.at[i])
        for i, (src, dst) in enumerate(
            (
                (q_hbm, q_ref),
                (k_hbm, k_ref),
                (v_hbm, v_ref),
                (decay_hbm, decay_ref),
                (rate_hbm, rate_ref),
                (gate_hbm, gate_ref),
                (cache_hbm, cache_ref),
            )
        )
    ]
    for load in loads:
        load.start()

    def columns(index):
        return pl.ds(pl.multiple_of(index * width, width), width)

    weight_loads = [
        pltpu.make_async_copy(
            proj_hbm.at[:, columns(index)],
            weight_ref.at[way, 0, :, pl.ds(part * width, width)],
            weight_load_sem.at[way, part],
        )
        for way in range(2)
        for part, index in enumerate((tensor, paired(tensor, 1 - way)))
    ]
    for load in weight_loads:
        load.start()

    lane = iota((8, 128), 1)
    block = jnp.zeros((8, 128), jnp.int32)
    for part, ref in enumerate((owner_ref, node_ref, prefix_ref, slot_ref)):
        for i in range(requests):
            block = jnp.where(lane == part * requests + i, ref[i], block)
    info_ref[...] = block

    barrier = pltpu.get_barrier_semaphore()
    for device in near + [(worker, index) for index in others]:
        pl.semaphore_signal(barrier, inc=1, device_id=device, device_id_type=MESH)
    pl.semaphore_wait(barrier, len(near) + len(others))

    def opposite(n):
        return n ^ 1

    infos = [
        remote(info_ref, told_ref.at[opposite(n)], info_send.at[n], info_recv.at[opposite(n)], near[n])
        for n in range(4)
    ]
    for copy in infos:
        copy.start()

    weights = []
    for kind in (MATE, CROSS, TWIN):
        for part in range(2):
            for way in range(2):
                index = sides[way][kind]
                target = paired(index, 1 - way) if part else index
                weights.append(
                    remote(
                        proj_hbm.at[:, columns(target)],
                        weight_ref.at[way, kind + 1, :, pl.ds(part * width, width)],
                        weight_send.at[way, kind, part],
                        weight_recv.at[way, kind, part],
                        (worker, index),
                    )
                )
    for copy in weights:
        copy.start()

    def hop(way, i):
        return remote(
            hop_out_ref.at[way, i], hop_in_ref.at[way, i], hop_send.at[way, i], hop_recv.at[way, i], near[2 + way]
        )

    def lend(way, i):
        return remote(
            lent_ref.at[way, i], borrowed_ref.at[way, i], lend_send.at[way, i], lend_recv.at[way, i], near[2 + way]
        )

    def send_end(way, i):
        return remote(
            sent_end_ref.at[i], got_end_ref.at[2 + way, i], end_send.at[2 + way, i], end_recv.at[2 + way, i], near[2 + way]
        )

    def pass_end(way, i):
        return remote(
            got_end_ref.at[2 + way, i], got_end_ref.at[way, i], end_send.at[way, i], end_recv.at[way, i], near[2 + way]
        )

    def send_normed(kind, i):
        source = 2 if kind == CROSS else 0
        index = sides[i % 2][MATE] if kind == MATE else twin
        return remote(
            normed_ref.at[i, source],
            normed_ref.at[i, kind + 1],
            normed_send.at[kind, i],
            normed_recv.at[kind, i],
            (worker, index),
        )

    def send_partial(i):
        index = sides[1 - i % 2][MATE]
        return remote(passed_ref.at[i], got_ref.at[i], partial_send.at[i], partial_recv.at[i], (worker, index))

    def wanted(n, i):
        return cache_ref[jnp.clip(told_smem[n, 0, requests + i], 0, slots - 1)].astype(jnp.bfloat16)

    def answer():
        for n in range(4):
            remote(info_ref, told_ref.at[n], info_send.at[n], info_recv.at[n], near[n]).wait_recv()
        fetch = pltpu.make_async_copy(told_ref, told_smem, told_sem)
        fetch.start()
        fetch.wait()
        loads[6].wait()
        for i in range(requests):
            for way in range(2):
                hop_out_ref[way, i] = wanted(way, i)
                hop(way, i).start()

    def merge(i):
        for way in range(2):
            hop(way, i).wait_recv()
            mine = told_smem[2 + way, 0, i] == worker
            lent_ref[way, i] = jnp.where(mine, wanted(2 + way, i), hop_in_ref[way, i])
            lend(way, i).start()

    def complete(i):
        for way in range(2):
            lend(way, i).wait_recv()
        move = lax.rem(owner_ref[i] - worker + workers + REACH, workers) - REACH
        node = jnp.clip(node_ref[i], 0, slots - 1)
        cached = prefix_ref[i] > 0
        starts = []
        for h in range(heads):
            start = cache_ref[node, h].astype(jnp.bfloat16)
            start = jnp.where(move < 0, borrowed_ref[1, i, h], start)
            start = jnp.where(move > 0, borrowed_ref[0, i, h], start)
            starts.append(jnp.where(cached, start, jnp.zeros_like(start)))
        slots_here = [i * heads + h for h in range(heads)]
        normed, ends = finish(slots_here, starts, zhi_ref, zlo_ref, base_ref, gain_gate_ref)
        for h in range(heads):
            normed_ref[i, 0, :, h * DV : (h + 1) * DV] = normed[h]
            sent_end_ref[i, h] = ends[h].astype(jnp.bfloat16)
        send_normed(MATE, i).start()
        send_normed(TWIN, i).start()
        for way in range(2):
            send_end(way, i).start()

    def relay(i):
        for way in range(2):
            send_end(way, i).wait_recv()
            pass_end(way, i).start()

    def forward(i):
        send_normed(MATE, i).wait_recv()
        send_normed(CROSS, i).start()

    def project(i):
        send_normed(TWIN, i).wait_recv()
        send_normed(CROSS, i).wait_recv()
        way = i % 2
        total = dot1(normed_ref[i, 0], weight_ref[way, 0])
        for source in range(1, 4):
            total = total + dot1(normed_ref[i, source], weight_ref[way, source])
        kept_ref[i] = total[:, :width]
        passed_ref[i] = total[:, width:].astype(jnp.bfloat16)
        send_partial(i).start()

    def add(i):
        send_partial(i).wait_recv()
        mixed_ref[i] = (kept_ref[i] + got_ref[i].astype(jnp.float32)).astype(jnp.bfloat16)

    for load in loads[:6]:
        load.wait()

    def ready(rs, between):
        prepare(
            rs, between, q_ref, k_ref, v_ref, gate_ref, decay_ref, rate_ref, gain_ref, zhi_ref, zlo_ref, base_ref, gain_gate_ref
        )

    def merge_first():
        merge(0)
        merge(1)

    ready([0, 1], answer)
    ready([2, 3], merge_first)
    merge(2)
    merge(3)
    complete(0)
    complete(1)
    complete(2)
    complete(3)
    for load in weight_loads:
        load.wait()
    for copy in weights:
        copy.wait_recv()
    relay(0)
    forward(0)
    relay(1)
    forward(1)
    project(0)
    relay(2)
    project(1)
    forward(2)
    relay(3)
    forward(3)
    project(2)
    project(3)
    add(0)
    add(1)
    add(2)
    for i in range(requests):
        for way in range(2):
            pass_end(way, i).wait_recv()
    for target in range(requests):
        row = worker * requests + target
        mine, theirs = jnp.int32(0), jnp.int32(0)
        kept = jnp.bool_(False)
        for i in range(requests):
            here = slot_ref[i] == row
            kept = kept | here
            mine = jnp.where(here, i, mine)
            for n in range(4):
                theirs = jnp.where(told_smem[opposite(n), 0, 3 * requests + i] == row, n * requests + i, theirs)
        end_ref[target] = jnp.where(
            kept, sent_end_ref[mine], got_end_ref[theirs // requests, theirs % requests]
        )
    add(3)

    for copy in infos + weights:
        copy.wait_send()
    for i in range(requests):
        for way in range(2):
            hop(way, i).wait_send()
            lend(way, i).wait_send()
            send_end(way, i).wait_send()
            pass_end(way, i).wait_send()
        for kind in (TWIN, MATE, CROSS):
            send_normed(kind, i).wait_send()
        send_partial(i).wait_send()


def store_kernel(mixed_ref, end_ref, mixed_hbm, end_hbm, wide_ref, mixed_sem, end_sem):
    requests = mixed_ref.shape[0]
    copies = [pltpu.make_async_copy(mixed_ref.at[i], mixed_hbm.at[i], mixed_sem.at[i]) for i in range(requests)]
    for copy in copies:
        copy.start()
    for i in range(requests):
        wide_ref[i] = end_ref[i].astype(jnp.float32)
        copies.append(pltpu.make_async_copy(wide_ref.at[i], end_hbm.at[i], end_sem.at[i]))
        copies[-1].start()
    for copy in copies:
        copy.wait()


def on_device(
    queries,
    key_heads,
    values_in,
    out_gate,
    log_decay,
    write_rate,
    cache_states,
    norm_gain,
    out_proj,
    hit_owner,
    hit_node,
    prefix_len,
    write_slot,
):
    requests, tokens = queries.shape[:2]
    heads = log_decay.shape[1]
    width = heads * DV
    state = cache_states.shape[1:]
    smem = pl.BlockSpec(memory_space=pltpu.SMEM)
    vmem = pl.BlockSpec(memory_space=pltpu.VMEM)
    anywhere = pl.BlockSpec(memory_space=pltpu.HBM)
    low, wide = jnp.bfloat16, jnp.float32
    dma = pltpu.SemaphoreType.DMA
    mixed, ends = pl.pallas_call(
        functools.partial(layer_kernel, lax.axis_size("worker")),
        out_shape=(
            pltpu.VMEM((requests, tokens, width), low),
            pltpu.VMEM((requests, *state), low),
        ),
        in_specs=[smem] * 4 + [vmem] + [anywhere] * 8,
        out_specs=(vmem, vmem),
        scratch_shapes=[
            pltpu.VMEM(queries.shape, low),
            pltpu.VMEM(key_heads.shape, low),
            pltpu.VMEM(values_in.shape, low),
            pltpu.VMEM(out_gate.shape, low),
            pltpu.VMEM(log_decay.shape, wide),
            pltpu.VMEM(write_rate.shape, wide),
            pltpu.VMEM(cache_states.shape, wide),
            pltpu.VMEM((requests * heads, tokens + DK, DK), low),
            pltpu.VMEM((requests * heads, tokens + DK, DK), low),
            pltpu.VMEM((requests * heads, tokens + DK, DV), wide),
            pltpu.VMEM((requests * heads, tokens, DV), wide),
            pltpu.VMEM((8, 128), jnp.int32),
            pltpu.VMEM((4, 8, 128), jnp.int32),
            pltpu.SMEM((4, 8, 128), jnp.int32),
            pltpu.VMEM((2, requests, *state), low),
            pltpu.VMEM((2, requests, *state), low),
            pltpu.VMEM((2, requests, *state), low),
            pltpu.VMEM((2, requests, *state), low),
            pltpu.VMEM((requests, *state), low),
            pltpu.VMEM((4, requests, *state), low),
            pltpu.VMEM((2, 4, width, 2 * width), low),
            pltpu.VMEM((requests, 4, tokens, width), low),
            pltpu.VMEM((requests, tokens, width), wide),
            pltpu.VMEM((requests, tokens, width), low),
            pltpu.VMEM((requests, tokens, width), low),
            dma((7,)),
            dma((2, 2)),
            dma,
            dma((4,)),
            dma((4,)),
            dma((2, requests)),
            dma((2, requests)),
            dma((2, requests)),
            dma((2, requests)),
            dma((4, requests)),
            dma((4, requests)),
            dma((2, 3, 2)),
            dma((2, 3, 2)),
            dma((3, requests)),
            dma((3, requests)),
            dma((requests,)),
            dma((requests,)),
        ],
        compiler_params=pltpu.CompilerParams(
            collective_id=0, has_side_effects=True, vmem_limit_bytes=48 * 1024 * 1024
        ),
        name="layer",
    )(
        *(
            pltpu.with_memory_space_constraint(x, pltpu.HBM)
            for x in (
                hit_owner,
                hit_node,
                prefix_len,
                write_slot,
                norm_gain[None],
                queries,
                key_heads,
                values_in,
                out_gate,
                log_decay,
                write_rate,
                cache_states,
                out_proj,
            )
        )
    )
    return pl.pallas_call(
        store_kernel,
        out_shape=(jax.ShapeDtypeStruct(mixed.shape, low), jax.ShapeDtypeStruct(ends.shape, wide)),
        in_specs=[vmem] * 2,
        out_specs=(anywhere, anywhere),
        scratch_shapes=[pltpu.VMEM(ends.shape, wide), dma((requests,)), dma((requests,))],
        compiler_params=pltpu.CompilerParams(vmem_limit_bytes=32 * 1024 * 1024),
        name="store",
    )(mixed, ends)


def solution(mesh):
    in_specs = (
        P("worker", None, "tensor"),
        P("worker", None, "tensor"),
        P("worker", None, "tensor"),
        P("worker", None, "tensor"),
        P("worker", "tensor", None),
        P("worker", "tensor", None),
        P("worker", "tensor", None, None),
        P(),
        P("tensor", None),
        P("worker"),
        P("worker"),
        P("worker"),
        P("worker"),
    )
    out_specs = (P("worker", None, "tensor"), P("worker", "tensor", None, None))
    return jax.shard_map(
        on_device, mesh=mesh, in_specs=in_specs, out_specs=out_specs, check_vma=False
    )
```

```python
import functools

import jax
import jax.numpy as jnp
from jax import lax
from jax.experimental import pallas as pl
from jax.experimental.pallas import tpu as pltpu
from jax.sharding import PartitionSpec as P

DK = 128
DV = 128
REACH = 2
SMALL = 8
MESH = pl.DeviceIdType.MESH
OFFSETS = (-2, 2, -1, 1)
TWIN, MATE, CROSS = range(3)


def split(x):
    hi = x.astype(jnp.bfloat16)
    return hi, (x - hi.astype(jnp.float32)).astype(jnp.bfloat16)


def dot1(a, b):
    return jnp.dot(a, b, preferred_element_type=jnp.float32)


def dot3(a, b):
    (a_hi, a_lo), (b_hi, b_lo) = a, b
    return dot1(jnp.concatenate([a_hi, a_lo, a_hi], axis=1), jnp.concatenate([b_hi, b_hi, b_lo], axis=0))


def dot_nt(a, b):
    return lax.dot_general(a, b, (((1,), (1,)), ((), ())), preferred_element_type=jnp.float32)


def dot_tn(a, b):
    return lax.dot_general(a, b, (((0,), (0,)), ((), ())), preferred_element_type=jnp.float32)


def iota(shape, dim):
    return lax.broadcasted_iota(jnp.int32, shape, dim)


def solve_small(compact):
    rows, lanes = compact.shape
    place = iota((rows, lanes), 1) % SMALL
    inverse = jnp.where(place == iota((rows, lanes), 0) % SMALL, 1.0, 0.0)
    for j in range(SMALL - 1):
        column = jnp.where(place == j, compact, 0.0)
        if j:
            column = pltpu.roll(column, lanes - j, 1)
        for step in (1, 2, 4):
            column = column + pltpu.roll(column, step, 1)
        groups = inverse.reshape(rows // SMALL, SMALL, lanes)
        row = jnp.broadcast_to(groups[:, j : j + 1, :], groups.shape).reshape(rows, lanes)
        inverse = inverse - column * row
    return inverse


def invert_unit_lower(systems):
    n = systems[0].shape[0]
    own = iota((n, n), 1) // SMALL == iota((n, n), 0) // SMALL
    compact = [
        jnp.sum(jnp.where(own, system, 0.0).reshape(n // SMALL, SMALL, n), axis=0) for system in systems
    ]
    small = solve_small(jnp.concatenate(compact, axis=0))
    inverses = []
    for i in range(len(systems)):
        block = small[i * SMALL : (i + 1) * SMALL]
        wide = jnp.broadcast_to(block[None], (n // SMALL, SMALL, n)).reshape(n, n)
        inverses.append(jnp.where(own, wide, 0.0))
    parts = [split(system) for system in systems]
    size = SMALL
    while size < n:
        row, lane = iota((n, n), 0) // size, iota((n, n), 1) // size
        below = (row % 2 == 1) & (row == lane + 1)
        cut = [tuple(jnp.where(below, part, jnp.zeros_like(part)) for part in pair) for pair in parts]
        halves = [split(inverse) for inverse in inverses]
        inner = [split(dot3(x, y)) for x, y in zip(cut, halves)]
        inverses = [inverse - dot3(x, y) for inverse, x, y in zip(inverses, halves, inner)]
        size *= 2
    return inverses


def prepare(
    rs, between, q_ref, k_ref, v_ref, gate_ref, decay_ref, rate_ref, gain_ref, zhi_ref, zlo_ref, base_ref, gain_gate_ref
):
    tokens = q_ref.shape[1]
    heads = decay_ref.shape[1]
    half = tokens // 2
    row, lane = iota((half, half), 0), iota((half, half), 1)
    upto = jnp.where(iota((tokens, tokens), 0) <= iota((tokens, tokens), 1), 1.0, 0.0).astype(jnp.bfloat16)
    decay = jnp.concatenate([decay_ref[r] for r in rs], axis=0)
    hi, _ = split(decay)
    rest = decay - hi.astype(jnp.float32)
    mid, low = split(rest)
    sums = dot1(jnp.concatenate([hi, mid, low], axis=0), upto)
    count = len(rs) * heads
    runnings = sums[2 * count :] + sums[count : 2 * count] + sums[:count]
    every = [runnings] + [rate_ref[r] for r in rs]
    pad = -2 * count % 8
    if pad:
        every.append(jnp.zeros((pad, tokens), jnp.float32))
    columns = jnp.concatenate(every, axis=0).T
    chains = []
    for n, r in enumerate(rs):
        q, k = q_ref[r], k_ref[r]
        qf, kf = q.astype(jnp.float32), k.astype(jnp.float32)
        rq = lax.rsqrt(jnp.sum(qf * qf, axis=1, keepdims=True) + 1e-06) * DK ** (-0.5)
        rk = lax.rsqrt(jnp.sum(kf * kf, axis=1, keepdims=True) + 1e-06)
        first, second = dot_nt(k, k[:half]), dot_nt(k[half:], k[half:])
        scales = [
            lax.rsqrt(jnp.sum(jnp.where(row == lane, raw, 0.0), axis=0, keepdims=True) + 1e-06)
            for raw in (first[:half], second)
        ]
        kk = [
            first[:half] * (scales[0] * rk[:half]),
            first[half:] * (scales[0] * rk[half:]),
            second * (scales[1] * rk[half:]),
        ]
        first, second = dot_nt(q, k[:half]), dot_nt(q[half:], k[half:])
        qk = [
            first[:half] * (scales[0] * rq[:half]),
            first[half:] * (scales[0] * rq[half:]),
            second * (scales[1] * rq[half:]),
        ]
        for h in range(heads):
            c = n * heads + h
            chains.append((r, h, qf, kf, rq, rk, kk, qk, columns[:, c : c + 1], columns[:, count + c : count + c + 1], runnings[c : c + 1]))
    systems, crosses, reads = [], [], []
    for r, h, qf, kf, rq, rk, kk, qk, g, rate, ahead in chains:
        within = [
            jnp.exp(jnp.where(row >= lane, g[:half] - ahead[:, :half], -jnp.inf)),
            jnp.exp(g[half:] - ahead[:, :half]),
            jnp.exp(jnp.where(row >= lane, g[half:] - ahead[:, half:], -jnp.inf)),
        ]
        systems.append(jnp.where(row > lane, rate[:half] * (within[0] * kk[0]), 0.0))
        systems.append(jnp.where(row > lane, rate[half:] * (within[2] * kk[2]), 0.0))
        crosses.append(split(rate[half:] * (within[1] * kk[1])))
        reads.append([split(x * y) for x, y in zip(within, qk)])
    inverses = [split(x) for x in invert_unit_lower(systems)]
    between()
    rights = []
    for r, h, qf, kf, rq, rk, kk, qk, g, rate, ahead in chains:
        values = v_ref[r, :, h * DV : (h + 1) * DV].astype(jnp.float32)
        rights.append(jnp.concatenate([rate * values, (rate * jnp.exp(g) * rk) * kf], axis=1))
    tops = [split(dot3(x, split(y[:half]))) for x, y in zip(inverses[::2], rights)]
    rests = [y[half:] - dot3(x, top) for x, y, top in zip(crosses, rights, tops)]
    bottoms = [split(dot3(x, split(rest))) for x, rest in zip(inverses[1::2], rests)]
    solveds = [
        tuple(jnp.concatenate([x, y], axis=0) for x, y in zip(top, bottom)) for top, bottom in zip(tops, bottoms)
    ]
    read_tops = [dot3(read[0], top) for read, top in zip(reads, tops)]
    read_bottoms = [
        dot3(tuple(jnp.concatenate([x, y], axis=1) for x, y in zip(read[1], read[2])), solved)
        for read, solved in zip(reads, solveds)
    ]
    ends = []
    for (r, h, qf, kf, rq, rk, kk, qk, g, rate, ahead), solved in zip(chains, solveds):
        hi, lo = split((jnp.exp(g[tokens - 1 :] - g) * rk) * kf)
        ends.append(dot_tn(jnp.concatenate([hi, lo, hi], axis=0), jnp.concatenate([solved[0], solved[0], solved[1]], axis=0)))
    eye = iota((DK, DK), 0) == iota((DK, DK), 1)
    for (r, h, qf, kf, rq, rk, kk, qk, g, rate, ahead), top, bottom, end in zip(chains, read_tops, read_bottoms, ends):
        slot = r * heads + h
        base_ref[slot, :half] = top[:, :DV]
        base_ref[slot, half:tokens] = bottom[:, :DV]
        base_ref[slot, tokens:] = end[:, :DV]
        from_state = (jnp.exp(g) * rq) * qf - jnp.concatenate([top[:, DV:], bottom[:, DV:]], axis=0)
        to_state = jnp.where(eye, jnp.exp(g[tokens - 1 :]), 0.0) - end[:, DV:]
        z_hi, z_lo = split(jnp.concatenate([from_state, to_state], axis=0))
        zhi_ref[slot] = z_hi
        zlo_ref[slot] = z_lo
        gate = gate_ref[r, :, h * DV : (h + 1) * DV].astype(jnp.float32)
        gain_gate_ref[slot] = gain_ref[...] * (gate / (1.0 + jnp.exp(-gate)))


def finish(slots, starts, zhi_ref, zlo_ref, base_ref, gain_gate_ref):
    tokens = gain_gate_ref.shape[1]
    wholes = [
        dot1(zhi_ref[slot], start) + dot1(zlo_ref[slot], start) + base_ref[slot] for slot, start in zip(slots, starts)
    ]
    scales = [
        lax.rsqrt(jnp.mean(whole[:tokens] * whole[:tokens], axis=1, keepdims=True) + 1e-06) for whole in wholes
    ]
    normed = [
        (whole[:tokens] * scale * gain_gate_ref[slot]).astype(jnp.bfloat16)
        for slot, whole, scale in zip(slots, wholes, scales)
    ]
    return normed, [whole[tokens:] for whole in wholes]


def layer_kernel(
    workers,
    owner_hbm,
    node_hbm,
    prefix_hbm,
    slot_hbm,
    gain_hbm,
    q_hbm,
    k_hbm,
    v_hbm,
    gate_hbm,
    decay_hbm,
    rate_hbm,
    cache_hbm,
    proj_hbm,
    mixed_ref,
    end_ref,
    owner_ref,
    node_ref,
    prefix_ref,
    slot_ref,
    gain_ref,
    q_ref,
    k_ref,
    v_ref,
    gate_ref,
    decay_ref,
    rate_ref,
    cache_ref,
    zhi_ref,
    zlo_ref,
    base_ref,
    gain_gate_ref,
    info_ref,
    told_ref,
    told_smem,
    hop_out_ref,
    hop_in_ref,
    lent_ref,
    borrowed_ref,
    sent_end_ref,
    got_end_ref,
    weight_ref,
    normed_ref,
    kept_ref,
    passed_ref,
    got_ref,
    ask_sem,
    load_sem,
    weight_load_sem,
    told_sem,
    info_send,
    info_recv,
    hop_send,
    hop_recv,
    lend_send,
    lend_recv,
    end_send,
    end_recv,
    weight_send,
    weight_recv,
    normed_send,
    normed_recv,
    partial_send,
    partial_recv,
):
    requests, tokens = q_ref.shape[:2]
    half = tokens // 2
    heads = decay_ref.shape[1]
    width = heads * DV
    slots = cache_ref.shape[0]
    worker = lax.axis_index("worker")
    tensor = lax.axis_index("tensor")
    chip, core = tensor // 2, tensor % 2

    def paired(index, way):
        there = index // 2
        mate = 3 - there if way else there + 1 - 2 * (there % 2)
        return 2 * mate + index % 2

    near = [(lax.rem(worker + workers + o, workers), tensor) for o in OFFSETS]
    twin = 2 * chip + 1 - core
    sides = [(twin, paired(tensor, way), paired(twin, way)) for way in range(2)]
    others = [twin, *sides[0][1:], *sides[1][1:]]

    def remote(src, dst, send, recv, device):
        return pltpu.make_async_remote_copy(
            src_ref=src, dst_ref=dst, send_sem=send, recv_sem=recv, device_id=device, device_id_type=MESH
        )

    barrier = pltpu.get_barrier_semaphore()
    for device in near + [(worker, index) for index in others]:
        pl.semaphore_signal(barrier, inc=1, device_id=device, device_id_type=MESH)
    asks = [
        pltpu.make_async_copy(src, dst, ask_sem.at[i])
        for i, (src, dst) in enumerate(
            ((owner_hbm, owner_ref), (node_hbm, node_ref), (prefix_hbm, prefix_ref), (slot_hbm, slot_ref))
        )
    ]
    for ask in asks:
        ask.start()
    loads = [
        pltpu.make_async_copy(src, dst, load_sem.at[i])
        for i, (src, dst) in enumerate(
            (
                (q_hbm, q_ref),
                (k_hbm, k_ref),
                (v_hbm, v_ref),
                (decay_hbm, decay_ref),
                (rate_hbm, rate_ref),
                (gate_hbm, gate_ref),
                (cache_hbm, cache_ref),
                (gain_hbm, gain_ref),
            )
        )
    ]
    for load in loads:
        load.start()

    def columns(index):
        return pl.ds(pl.multiple_of(index * width, width), width)

    weight_loads = [
        pltpu.make_async_copy(
            proj_hbm.at[:, columns(index)],
            weight_ref.at[way, 0, :, pl.ds(part * width, width)],
            weight_load_sem.at[way, part],
        )
        for way in range(2)
        for part, index in enumerate((tensor, paired(tensor, 1 - way)))
    ]
    for load in weight_loads:
        load.start()

    for ask in asks:
        ask.wait()
    lane = iota((8, 128), 1)
    block = jnp.zeros((8, 128), jnp.int32)
    for part, ref in enumerate((owner_ref, node_ref, prefix_ref, slot_ref)):
        for i in range(requests):
            block = jnp.where(lane == part * requests + i, ref[i], block)
    info_ref[...] = block

    pl.semaphore_wait(barrier, len(near) + len(others))

    def opposite(n):
        return n ^ 1

    infos = [
        remote(info_ref, told_ref.at[opposite(n)], info_send.at[n], info_recv.at[opposite(n)], near[n])
        for n in range(4)
    ]
    for copy in infos:
        copy.start()

    weights = []
    for kind in (MATE, CROSS, TWIN):
        for part in range(2):
            for way in range(2):
                index = sides[way][kind]
                target = paired(index, 1 - way) if part else index
                weights.append(
                    remote(
                        proj_hbm.at[:, columns(target)],
                        weight_ref.at[way, kind + 1, :, pl.ds(part * width, width)],
                        weight_send.at[way, kind, part],
                        weight_recv.at[way, kind, part],
                        (worker, index),
                    )
                )
    for copy in weights:
        copy.start()

    def hop(way, i):
        return remote(
            hop_out_ref.at[way, i], hop_in_ref.at[way, i], hop_send.at[way, i], hop_recv.at[way, i], near[2 + way]
        )

    def lend(way, i):
        return remote(
            lent_ref.at[way, i], borrowed_ref.at[way, i], lend_send.at[way, i], lend_recv.at[way, i], near[2 + way]
        )

    def send_end(way, i):
        return remote(
            sent_end_ref.at[i], got_end_ref.at[2 + way, i], end_send.at[2 + way, i], end_recv.at[2 + way, i], near[2 + way]
        )

    def pass_end(way, i):
        return remote(
            got_end_ref.at[2 + way, i], got_end_ref.at[way, i], end_send.at[way, i], end_recv.at[way, i], near[2 + way]
        )

    def rows(way):
        return pl.ds(way * half, half)

    def send_normed(kind, i, way):
        source = 2 if kind == CROSS else 0
        index = sides[way][MATE] if kind == MATE else twin
        return remote(
            normed_ref.at[i, source, rows(way)],
            normed_ref.at[i, kind + 1, rows(way)],
            normed_send.at[kind, i, way],
            normed_recv.at[kind, i, way],
            (worker, index),
        )

    def send_partial(i, way):
        index = sides[1 - way][MATE]
        return remote(
            passed_ref.at[i, rows(way)],
            got_ref.at[i, rows(way)],
            partial_send.at[i, way],
            partial_recv.at[i, way],
            (worker, index),
        )

    def wanted(n, i):
        return cache_ref[jnp.clip(told_smem[n, 0, requests + i], 0, slots - 1)].astype(jnp.bfloat16)

    def answer():
        for n in range(4):
            remote(info_ref, told_ref.at[n], info_send.at[n], info_recv.at[n], near[n]).wait_recv()
        fetch = pltpu.make_async_copy(told_ref, told_smem, told_sem)
        fetch.start()
        fetch.wait()
        loads[6].wait()
        for i in range(requests):
            for way in range(2):
                hop_out_ref[way, i] = wanted(way, i)
                hop(way, i).start()

    def merge(i):
        for way in range(2):
            hop(way, i).wait_recv()
            mine = told_smem[2 + way, 0, i] == worker
            lent_ref[way, i] = jnp.where(mine, wanted(2 + way, i), hop_in_ref[way, i])
            lend(way, i).start()

    def complete(i):
        for way in range(2):
            lend(way, i).wait_recv()
        move = lax.rem(owner_ref[i] - worker + workers + REACH, workers) - REACH
        node = jnp.clip(node_ref[i], 0, slots - 1)
        cached = prefix_ref[i] > 0
        starts = []
        for h in range(heads):
            start = cache_ref[node, h].astype(jnp.bfloat16)
            start = jnp.where(move < 0, borrowed_ref[1, i, h], start)
            start = jnp.where(move > 0, borrowed_ref[0, i, h], start)
            starts.append(jnp.where(cached, start, jnp.zeros_like(start)))
        slots_here = [i * heads + h for h in range(heads)]
        normed, ends = finish(slots_here, starts, zhi_ref, zlo_ref, base_ref, gain_gate_ref)
        for h in range(heads):
            normed_ref[i, 0, :, h * DV : (h + 1) * DV] = normed[h]
            sent_end_ref[i, h] = ends[h].astype(jnp.bfloat16)
        for kind in (MATE, TWIN):
            for way in range(2):
                send_normed(kind, i, way).start()
        for way in range(2):
            send_end(way, i).start()

    def relay(i):
        for way in range(2):
            send_end(way, i).wait_recv()
            pass_end(way, i).start()

    def forward(i):
        for way in range(2):
            send_normed(MATE, i, way).wait_recv()
            send_normed(CROSS, i, way).start()

    def project(i):
        for way in range(2):
            send_normed(TWIN, i, way).wait_recv()
            send_normed(CROSS, i, way).wait_recv()
            total = dot1(normed_ref[i, 0, rows(way)], weight_ref[way, 0])
            for source in range(1, 4):
                total = total + dot1(normed_ref[i, source, rows(way)], weight_ref[way, source])
            kept_ref[i, rows(way)] = total[:, :width]
            passed_ref[i, rows(way)] = total[:, width:].astype(jnp.bfloat16)
            send_partial(i, way).start()

    def add(i):
        for way in range(2):
            send_partial(i, way).wait_recv()
            mixed_ref[i, rows(way)] = (kept_ref[i, rows(way)] + got_ref[i, rows(way)].astype(jnp.float32)).astype(
                jnp.bfloat16
            )

    for load in loads[:6] + loads[7:]:
        load.wait()

    def ready(rs, between):
        prepare(
            rs, between, q_ref, k_ref, v_ref, gate_ref, decay_ref, rate_ref, gain_ref, zhi_ref, zlo_ref, base_ref, gain_gate_ref
        )

    def merge_first():
        merge(0)
        merge(1)

    ready([0, 1], answer)
    ready([2, 3], merge_first)
    merge(2)
    merge(3)
    complete(0)
    complete(1)
    complete(2)
    complete(3)
    for load in weight_loads:
        load.wait()
    for copy in weights:
        copy.wait_recv()
    forward(0)
    relay(0)
    forward(1)
    project(0)
    relay(1)
    forward(2)
    relay(2)
    project(1)
    relay(3)
    forward(3)
    project(2)
    project(3)
    add(0)
    add(1)
    add(2)
    add(3)
    for i in range(requests):
        for way in range(2):
            pass_end(way, i).wait_recv()
    for target in range(requests):
        row = worker * requests + target
        mine, theirs = jnp.int32(0), jnp.int32(0)
        kept = jnp.bool_(False)
        for i in range(requests):
            here = slot_ref[i] == row
            kept = kept | here
            mine = jnp.where(here, i, mine)
            for n in range(4):
                theirs = jnp.where(told_smem[opposite(n), 0, 3 * requests + i] == row, n * requests + i, theirs)
        end_ref[target] = jnp.where(
            kept, sent_end_ref[mine], got_end_ref[theirs // requests, theirs % requests]
        )

    for copy in infos + weights:
        copy.wait_send()
    for i in range(requests):
        for way in range(2):
            hop(way, i).wait_send()
            lend(way, i).wait_send()
            send_end(way, i).wait_send()
            pass_end(way, i).wait_send()
        for way in range(2):
            for kind in (TWIN, MATE, CROSS):
                send_normed(kind, i, way).wait_send()
            send_partial(i, way).wait_send()


def store_kernel(mixed_ref, end_ref, mixed_hbm, end_hbm, wide_ref, mixed_sem, end_sem):
    requests = mixed_ref.shape[0]
    copies = [pltpu.make_async_copy(mixed_ref.at[i], mixed_hbm.at[i], mixed_sem.at[i]) for i in range(requests)]
    for copy in copies:
        copy.start()
    for i in range(requests):
        wide_ref[i] = end_ref[i].astype(jnp.float32)
        copies.append(pltpu.make_async_copy(wide_ref.at[i], end_hbm.at[i], end_sem.at[i]))
        copies[-1].start()
    for copy in copies:
        copy.wait()


def on_device(
    queries,
    key_heads,
    values_in,
    out_gate,
    log_decay,
    write_rate,
    cache_states,
    norm_gain,
    out_proj,
    hit_owner,
    hit_node,
    prefix_len,
    write_slot,
):
    requests, tokens = queries.shape[:2]
    heads = log_decay.shape[1]
    width = heads * DV
    state = cache_states.shape[1:]
    vmem = pl.BlockSpec(memory_space=pltpu.VMEM)
    anywhere = pl.BlockSpec(memory_space=pltpu.HBM)
    low, wide = jnp.bfloat16, jnp.float32
    dma = pltpu.SemaphoreType.DMA
    mixed, ends = pl.pallas_call(
        functools.partial(layer_kernel, lax.axis_size("worker")),
        out_shape=(
            pltpu.VMEM((requests, tokens, width), low),
            pltpu.VMEM((requests, *state), low),
        ),
        in_specs=[anywhere] * 13,
        out_specs=(vmem, vmem),
        scratch_shapes=[
            *[pltpu.SMEM((requests,), jnp.int32)] * 4,
            pltpu.VMEM((1, DV), wide),
            pltpu.VMEM(queries.shape, low),
            pltpu.VMEM(key_heads.shape, low),
            pltpu.VMEM(values_in.shape, low),
            pltpu.VMEM(out_gate.shape, low),
            pltpu.VMEM(log_decay.shape, wide),
            pltpu.VMEM(write_rate.shape, wide),
            pltpu.VMEM(cache_states.shape, wide),
            pltpu.VMEM((requests * heads, tokens + DK, DK), low),
            pltpu.VMEM((requests * heads, tokens + DK, DK), low),
            pltpu.VMEM((requests * heads, tokens + DK, DV), wide),
            pltpu.VMEM((requests * heads, tokens, DV), wide),
            pltpu.VMEM((8, 128), jnp.int32),
            pltpu.VMEM((4, 8, 128), jnp.int32),
            pltpu.SMEM((4, 8, 128), jnp.int32),
            pltpu.VMEM((2, requests, *state), low),
            pltpu.VMEM((2, requests, *state), low),
            pltpu.VMEM((2, requests, *state), low),
            pltpu.VMEM((2, requests, *state), low),
            pltpu.VMEM((requests, *state), low),
            pltpu.VMEM((4, requests, *state), low),
            pltpu.VMEM((2, 4, width, 2 * width), low),
            pltpu.VMEM((requests, 4, tokens, width), low),
            pltpu.VMEM((requests, tokens, width), wide),
            pltpu.VMEM((requests, tokens, width), low),
            pltpu.VMEM((requests, tokens, width), low),
            dma((4,)),
            dma((8,)),
            dma((2, 2)),
            dma,
            dma((4,)),
            dma((4,)),
            dma((2, requests)),
            dma((2, requests)),
            dma((2, requests)),
            dma((2, requests)),
            dma((4, requests)),
            dma((4, requests)),
            dma((2, 3, 2)),
            dma((2, 3, 2)),
            dma((3, requests, 2)),
            dma((3, requests, 2)),
            dma((requests, 2)),
            dma((requests, 2)),
        ],
        compiler_params=pltpu.CompilerParams(
            collective_id=0, has_side_effects=True, vmem_limit_bytes=48 * 1024 * 1024
        ),
        name="layer",
    )(
        *(
            pltpu.with_memory_space_constraint(x, pltpu.HBM)
            for x in (
                hit_owner,
                hit_node,
                prefix_len,
                write_slot,
                norm_gain[None],
                queries,
                key_heads,
                values_in,
                out_gate,
                log_decay,
                write_rate,
                cache_states,
                out_proj,
            )
        )
    )
    return pl.pallas_call(
        store_kernel,
        out_shape=(jax.ShapeDtypeStruct(mixed.shape, low), jax.ShapeDtypeStruct(ends.shape, wide)),
        in_specs=[vmem] * 2,
        out_specs=(anywhere, anywhere),
        scratch_shapes=[pltpu.VMEM(ends.shape, wide), dma((requests,)), dma((requests,))],
        compiler_params=pltpu.CompilerParams(vmem_limit_bytes=32 * 1024 * 1024),
        name="store",
    )(mixed, ends)


def solution(mesh):
    in_specs = (
        P("worker", None, "tensor"),
        P("worker", None, "tensor"),
        P("worker", None, "tensor"),
        P("worker", None, "tensor"),
        P("worker", "tensor", None),
        P("worker", "tensor", None),
        P("worker", "tensor", None, None),
        P(),
        P("tensor", None),
        P("worker"),
        P("worker"),
        P("worker"),
        P("worker"),
    )
    out_specs = (P("worker", None, "tensor"), P("worker", "tensor", None, None))
    return jax.shard_map(
        on_device, mesh=mesh, in_specs=in_specs, out_specs=out_specs, check_vma=False
    )
```

```python
import functools

import jax
import jax.numpy as jnp
from jax import lax
from jax.experimental import pallas as pl
from jax.experimental.pallas import tpu as pltpu
from jax.sharding import PartitionSpec as P

DK = 128
DV = 128
REACH = 2
SMALL = 8
MESH = pl.DeviceIdType.MESH
OFFSETS = (-2, 2, -1, 1)
TWIN = 0


def split(x):
    hi = x.astype(jnp.bfloat16)
    return hi, (x - hi.astype(jnp.float32)).astype(jnp.bfloat16)


def dot1(a, b):
    return jnp.dot(a, b, preferred_element_type=jnp.float32)


def dot3(a, b):
    (a_hi, a_lo), (b_hi, b_lo) = a, b
    return dot1(jnp.concatenate([a_hi, a_lo, a_hi], axis=1), jnp.concatenate([b_hi, b_hi, b_lo], axis=0))


def dot_nt(a, b):
    return lax.dot_general(a, b, (((1,), (1,)), ((), ())), preferred_element_type=jnp.float32)


def dot_tn(a, b):
    return lax.dot_general(a, b, (((0,), (0,)), ((), ())), preferred_element_type=jnp.float32)


def iota(shape, dim):
    return lax.broadcasted_iota(jnp.int32, shape, dim)


def solve_small(compact):
    rows, lanes = compact.shape
    place = iota((rows, lanes), 1) % SMALL
    inverse = jnp.where(place == iota((rows, lanes), 0) % SMALL, 1.0, 0.0)
    for j in range(SMALL - 1):
        column = jnp.where(place == j, compact, 0.0)
        if j:
            column = pltpu.roll(column, lanes - j, 1)
        for step in (1, 2, 4):
            column = column + pltpu.roll(column, step, 1)
        groups = inverse.reshape(rows // SMALL, SMALL, lanes)
        row = jnp.broadcast_to(groups[:, j : j + 1, :], groups.shape).reshape(rows, lanes)
        inverse = inverse - column * row
    return inverse


def invert_unit_lower(systems):
    n = systems[0].shape[0]
    own = iota((n, n), 1) // SMALL == iota((n, n), 0) // SMALL
    compact = [
        jnp.sum(jnp.where(own, system, 0.0).reshape(n // SMALL, SMALL, n), axis=0) for system in systems
    ]
    small = solve_small(jnp.concatenate(compact, axis=0))
    inverses = []
    for i in range(len(systems)):
        block = small[i * SMALL : (i + 1) * SMALL]
        wide = jnp.broadcast_to(block[None], (n // SMALL, SMALL, n)).reshape(n, n)
        inverses.append(jnp.where(own, wide, 0.0))
    parts = [split(system) for system in systems]
    size = SMALL
    while size < n:
        row, lane = iota((n, n), 0) // size, iota((n, n), 1) // size
        below = (row % 2 == 1) & (row == lane + 1)
        cut = [tuple(jnp.where(below, part, jnp.zeros_like(part)) for part in pair) for pair in parts]
        halves = [split(inverse) for inverse in inverses]
        inner = [split(dot3(x, y)) for x, y in zip(cut, halves)]
        inverses = [inverse - dot3(x, y) for inverse, x, y in zip(inverses, halves, inner)]
        size *= 2
    return inverses


def prepare(
    rs, between, q_ref, k_ref, v_ref, gate_ref, decay_ref, rate_ref, gain_ref, zhi_ref, zlo_ref, base_ref, gain_gate_ref
):
    tokens = q_ref.shape[1]
    heads = decay_ref.shape[1]
    half = tokens // 2
    row, lane = iota((half, half), 0), iota((half, half), 1)
    upto = jnp.where(iota((tokens, tokens), 0) <= iota((tokens, tokens), 1), 1.0, 0.0).astype(jnp.bfloat16)
    decay = jnp.concatenate([decay_ref[r] for r in rs], axis=0)
    hi, _ = split(decay)
    rest = decay - hi.astype(jnp.float32)
    mid, low = split(rest)
    sums = dot1(jnp.concatenate([hi, mid, low], axis=0), upto)
    count = len(rs) * heads
    runnings = sums[2 * count :] + sums[count : 2 * count] + sums[:count]
    every = [runnings] + [rate_ref[r] for r in rs]
    pad = -2 * count % 8
    if pad:
        every.append(jnp.zeros((pad, tokens), jnp.float32))
    columns = jnp.concatenate(every, axis=0).T
    chains = []
    for n, r in enumerate(rs):
        q, k = q_ref[r], k_ref[r]
        qf, kf = q.astype(jnp.float32), k.astype(jnp.float32)
        rq = lax.rsqrt(jnp.sum(qf * qf, axis=1, keepdims=True) + 1e-06) * DK ** (-0.5)
        rk = lax.rsqrt(jnp.sum(kf * kf, axis=1, keepdims=True) + 1e-06)
        first, second = dot_nt(k, k[:half]), dot_nt(k[half:], k[half:])
        scales = [
            lax.rsqrt(jnp.sum(jnp.where(row == lane, raw, 0.0), axis=0, keepdims=True) + 1e-06)
            for raw in (first[:half], second)
        ]
        kk = [
            first[:half] * (scales[0] * rk[:half]),
            first[half:] * (scales[0] * rk[half:]),
            second * (scales[1] * rk[half:]),
        ]
        first, second = dot_nt(q, k[:half]), dot_nt(q[half:], k[half:])
        qk = [
            first[:half] * (scales[0] * rq[:half]),
            first[half:] * (scales[0] * rq[half:]),
            second * (scales[1] * rq[half:]),
        ]
        for h in range(heads):
            c = n * heads + h
            chains.append((r, h, qf, kf, rq, rk, kk, qk, columns[:, c : c + 1], columns[:, count + c : count + c + 1], runnings[c : c + 1]))
    systems, crosses, reads = [], [], []
    for r, h, qf, kf, rq, rk, kk, qk, g, rate, ahead in chains:
        within = [
            jnp.exp(jnp.where(row >= lane, g[:half] - ahead[:, :half], -jnp.inf)),
            jnp.exp(g[half:] - ahead[:, :half]),
            jnp.exp(jnp.where(row >= lane, g[half:] - ahead[:, half:], -jnp.inf)),
        ]
        systems.append(jnp.where(row > lane, rate[:half] * (within[0] * kk[0]), 0.0))
        systems.append(jnp.where(row > lane, rate[half:] * (within[2] * kk[2]), 0.0))
        crosses.append(split(rate[half:] * (within[1] * kk[1])))
        reads.append([split(x * y) for x, y in zip(within, qk)])
    inverses = [split(x) for x in invert_unit_lower(systems)]
    between()
    rights = []
    for r, h, qf, kf, rq, rk, kk, qk, g, rate, ahead in chains:
        values = v_ref[r, :, h * DV : (h + 1) * DV].astype(jnp.float32)
        rights.append(jnp.concatenate([rate * values, (rate * jnp.exp(g) * rk) * kf], axis=1))
    tops = [split(dot3(x, split(y[:half]))) for x, y in zip(inverses[::2], rights)]
    rests = [y[half:] - dot3(x, top) for x, y, top in zip(crosses, rights, tops)]
    bottoms = [split(dot3(x, split(rest))) for x, rest in zip(inverses[1::2], rests)]
    solveds = [
        tuple(jnp.concatenate([x, y], axis=0) for x, y in zip(top, bottom)) for top, bottom in zip(tops, bottoms)
    ]
    read_tops = [dot3(read[0], top) for read, top in zip(reads, tops)]
    read_bottoms = [
        dot3(tuple(jnp.concatenate([x, y], axis=1) for x, y in zip(read[1], read[2])), solved)
        for read, solved in zip(reads, solveds)
    ]
    ends = []
    for (r, h, qf, kf, rq, rk, kk, qk, g, rate, ahead), solved in zip(chains, solveds):
        hi, lo = split((jnp.exp(g[tokens - 1 :] - g) * rk) * kf)
        ends.append(dot_tn(jnp.concatenate([hi, lo, hi], axis=0), jnp.concatenate([solved[0], solved[0], solved[1]], axis=0)))
    eye = iota((DK, DK), 0) == iota((DK, DK), 1)
    for (r, h, qf, kf, rq, rk, kk, qk, g, rate, ahead), top, bottom, end in zip(chains, read_tops, read_bottoms, ends):
        slot = r * heads + h
        base_ref[slot, :half] = top[:, :DV]
        base_ref[slot, half:tokens] = bottom[:, :DV]
        base_ref[slot, tokens:] = end[:, :DV]
        from_state = (jnp.exp(g) * rq) * qf - jnp.concatenate([top[:, DV:], bottom[:, DV:]], axis=0)
        to_state = jnp.where(eye, jnp.exp(g[tokens - 1 :]), 0.0) - end[:, DV:]
        z_hi, z_lo = split(jnp.concatenate([from_state, to_state], axis=0))
        zhi_ref[slot] = z_hi
        zlo_ref[slot] = z_lo
        gate = gate_ref[r, :, h * DV : (h + 1) * DV].astype(jnp.float32)
        gain_gate_ref[slot] = gain_ref[...] * (gate / (1.0 + jnp.exp(-gate)))


def finish(slots, starts, zhi_ref, zlo_ref, base_ref, gain_gate_ref):
    tokens = gain_gate_ref.shape[1]
    wholes = [
        dot1(zhi_ref[slot], start) + dot1(zlo_ref[slot], start) + base_ref[slot] for slot, start in zip(slots, starts)
    ]
    scales = [
        lax.rsqrt(jnp.mean(whole[:tokens] * whole[:tokens], axis=1, keepdims=True) + 1e-06) for whole in wholes
    ]
    normed = [
        (whole[:tokens] * scale * gain_gate_ref[slot]).astype(jnp.bfloat16)
        for slot, whole, scale in zip(slots, wholes, scales)
    ]
    return normed, [whole[tokens:] for whole in wholes]


def layer_kernel(
    workers,
    owner_hbm,
    node_hbm,
    prefix_hbm,
    slot_hbm,
    gain_hbm,
    q_hbm,
    k_hbm,
    v_hbm,
    gate_hbm,
    decay_hbm,
    rate_hbm,
    cache_hbm,
    proj_hbm,
    mixed_ref,
    end_ref,
    owner_ref,
    node_ref,
    prefix_ref,
    slot_ref,
    gain_ref,
    q_ref,
    k_ref,
    v_ref,
    gate_ref,
    decay_ref,
    rate_ref,
    cache_ref,
    zhi_ref,
    zlo_ref,
    base_ref,
    gain_gate_ref,
    info_ref,
    told_ref,
    told_smem,
    hop_out_ref,
    hop_in_ref,
    lent_ref,
    borrowed_ref,
    sent_end_ref,
    got_end_ref,
    weight_ref,
    normed_ref,
    gathered_ref,
    kept_ref,
    passed_ref,
    got_ref,
    lent_sum_ref,
    twin_sum_ref,
    ask_sem,
    load_sem,
    weight_load_sem,
    told_sem,
    info_send,
    info_recv,
    hop_send,
    hop_recv,
    lend_send,
    lend_recv,
    end_send,
    end_recv,
    weight_send,
    weight_recv,
    normed_send,
    normed_recv,
    partial_send,
    partial_recv,
    swap_send,
    swap_recv,
):
    requests, tokens = q_ref.shape[:2]
    half = tokens // 2
    heads = decay_ref.shape[1]
    width = heads * DV
    slots = cache_ref.shape[0]
    worker = lax.axis_index("worker")
    tensor = lax.axis_index("tensor")
    chip, core = tensor // 2, tensor % 2

    def paired(there, way):
        return (1 - way) * (there + 1 - 2 * (there % 2)) + way * (3 - there)

    near = [(lax.rem(worker + workers + o, workers), tensor) for o in OFFSETS]
    twin = 2 * chip + 1 - core
    others = [twin] + [2 * paired(chip, way) + c for way in range(2) for c in range(2)]
    beyond = paired(chip, 1 - core)

    def remote(src, dst, send, recv, device):
        return pltpu.make_async_remote_copy(
            src_ref=src, dst_ref=dst, send_sem=send, recv_sem=recv, device_id=device, device_id_type=MESH
        )

    barrier = pltpu.get_barrier_semaphore()
    for device in near + [(worker, index) for index in others]:
        pl.semaphore_signal(barrier, inc=1, device_id=device, device_id_type=MESH)
    asks = [
        pltpu.make_async_copy(src, dst, ask_sem.at[i])
        for i, (src, dst) in enumerate(
            ((owner_hbm, owner_ref), (node_hbm, node_ref), (prefix_hbm, prefix_ref), (slot_hbm, slot_ref))
        )
    ]
    for ask in asks:
        ask.start()
    loads = [
        pltpu.make_async_copy(src, dst, load_sem.at[i])
        for i, (src, dst) in enumerate(
            (
                (q_hbm, q_ref),
                (k_hbm, k_ref),
                (v_hbm, v_ref),
                (decay_hbm, decay_ref),
                (rate_hbm, rate_ref),
                (gate_hbm, gate_ref),
                (cache_hbm, cache_ref),
                (gain_hbm, gain_ref),
            )
        )
    ]
    for load in loads:
        load.start()

    def columns(there):
        return pl.ds(pl.multiple_of(there * 2 * width, 2 * width), 2 * width)

    def rows(c):
        return pl.ds(pl.multiple_of(c * half, half), half)

    weight_loads = [
        pltpu.make_async_copy(
            proj_hbm.at[:, columns(there)],
            weight_ref.at[0, :, pl.ds(part * 2 * width, 2 * width)],
            weight_load_sem.at[part],
        )
        for part, there in enumerate((chip, beyond))
    ]
    for load in weight_loads:
        load.start()

    for ask in asks:
        ask.wait()
    lane = iota((8, 128), 1)
    block = jnp.zeros((8, 128), jnp.int32)
    for part, ref in enumerate((owner_ref, node_ref, prefix_ref, slot_ref)):
        for i in range(requests):
            block = jnp.where(lane == part * requests + i, ref[i], block)
    info_ref[...] = block

    pl.semaphore_wait(barrier, len(near) + len(others))

    def opposite(n):
        return n ^ 1

    infos = [
        remote(info_ref, told_ref.at[opposite(n)], info_send.at[n], info_recv.at[opposite(n)], near[n])
        for n in range(4)
    ]
    for copy in infos:
        copy.start()

    def route(kind):
        if kind == TWIN:
            return twin, 1, 1 - core, chip
        way = kind - 1
        there = paired(chip, way)
        return 2 * there + way, 2 + lax.rem(core + way, 2), way, there

    weights = []
    for kind in (1, 2, TWIN):
        index, source, way, there = route(kind)
        for part, block in enumerate((there, paired(there, 1 - way))):
            weights.append(
                remote(
                    proj_hbm.at[:, columns(block)],
                    weight_ref.at[source, :, pl.ds(part * 2 * width, 2 * width)],
                    weight_send.at[kind, part],
                    weight_recv.at[source - 1, part],
                    (worker, index),
                )
            )
    got_weights = [
        remote(
            proj_hbm.at[:, columns(chip)],
            weight_ref.at[source, :, pl.ds(part * 2 * width, 2 * width)],
            weight_send.at[source - 1, part],
            weight_recv.at[source - 1, part],
            (worker, twin),
        )
        for source in range(1, 4)
        for part in range(2)
    ]
    for copy in weights:
        copy.start()

    def hop(way, i):
        return remote(
            hop_out_ref.at[way, i], hop_in_ref.at[way, i], hop_send.at[way, i], hop_recv.at[way, i], near[2 + way]
        )

    def lend(way, i):
        return remote(
            lent_ref.at[way, i], borrowed_ref.at[way, i], lend_send.at[way, i], lend_recv.at[way, i], near[2 + way]
        )

    def send_end(way, i):
        return remote(
            sent_end_ref.at[i], got_end_ref.at[2 + way, i], end_send.at[2 + way, i], end_recv.at[2 + way, i], near[2 + way]
        )

    def pass_end(way, i):
        return remote(
            got_end_ref.at[2 + way, i], got_end_ref.at[way, i], end_send.at[way, i], end_recv.at[way, i], near[2 + way]
        )

    def send_normed(kind, i):
        index, source, way, _ = route(kind)
        return remote(
            normed_ref.at[i, rows(way)],
            gathered_ref.at[i, source - 1],
            normed_send.at[kind, i],
            normed_recv.at[source - 1, i],
            (worker, index),
        )

    def get_normed(source, i):
        return remote(
            normed_ref.at[i, rows(core)],
            gathered_ref.at[i, source - 1],
            normed_send.at[source - 1, i],
            normed_recv.at[source - 1, i],
            (worker, twin),
        )

    def send_partial(i, c):
        return remote(
            passed_ref.at[i, c],
            got_ref.at[i, rows(core)],
            partial_send.at[i, c],
            partial_recv.at[i, core],
            (worker, 2 * beyond + c),
        )

    def get_partial(i, c):
        return remote(
            passed_ref.at[i, c], got_ref.at[i, rows(c)], partial_send.at[i, c], partial_recv.at[i, c], (worker, twin)
        )

    def swap(i):
        return remote(lent_sum_ref.at[i], twin_sum_ref.at[i], swap_send.at[i], swap_recv.at[i], (worker, twin))

    def wanted(n, i):
        return cache_ref[jnp.clip(told_smem[n, 0, requests + i], 0, slots - 1)].astype(jnp.bfloat16)

    def answer():
        for n in range(4):
            remote(info_ref, told_ref.at[n], info_send.at[n], info_recv.at[n], near[n]).wait_recv()
        fetch = pltpu.make_async_copy(told_ref, told_smem, told_sem)
        fetch.start()
        fetch.wait()
        loads[6].wait()
        for i in range(requests):
            for way in range(2):
                hop_out_ref[way, i] = wanted(way, i)
                if i < requests - 1:
                    hop(way, i).start()

    def merge(i):
        for way in range(2):
            hop(way, i).wait_recv()
            mine = told_smem[2 + way, 0, i] == worker
            lent_ref[way, i] = jnp.where(mine, wanted(2 + way, i), hop_in_ref[way, i])
            lend(way, i).start()

    def complete(i):
        for way in range(2):
            lend(way, i).wait_recv()
        move = lax.rem(owner_ref[i] - worker + workers + REACH, workers) - REACH
        node = jnp.clip(node_ref[i], 0, slots - 1)
        cached = prefix_ref[i] > 0
        starts = []
        for h in range(heads):
            start = cache_ref[node, h].astype(jnp.bfloat16)
            start = jnp.where(move < 0, borrowed_ref[1, i, h], start)
            start = jnp.where(move > 0, borrowed_ref[0, i, h], start)
            starts.append(jnp.where(cached, start, jnp.zeros_like(start)))
        slots_here = [i * heads + h for h in range(heads)]
        normed, ends = finish(slots_here, starts, zhi_ref, zlo_ref, base_ref, gain_gate_ref)
        for h in range(heads):
            normed_ref[i, :, h * DV : (h + 1) * DV] = normed[h]
            sent_end_ref[i, h] = ends[h].astype(jnp.bfloat16)
        for kind in (1, 2, TWIN):
            send_normed(kind, i).start()
        for way in range(2):
            send_end(way, i).start()

    def relay(i):
        for way in range(2):
            send_end(way, i).wait_recv()
            pass_end(way, i).start()

    def project(i):
        total = dot1(normed_ref[i, rows(core)], weight_ref[0])
        for source in range(1, 4):
            get_normed(source, i).wait_recv()
            total = total + dot1(gathered_ref[i, source - 1], weight_ref[source])
        for c in range(2):
            passed_ref[i, c] = total[:, (2 + c) * width : (3 + c) * width].astype(jnp.bfloat16)
            send_partial(i, c).start()
        left, right = total[:, :width], total[:, width : 2 * width]
        lent_sum_ref[i] = jnp.where(core == 0, right, left).astype(jnp.bfloat16)
        swap(i).start()
        kept_ref[i] = jnp.where(core == 0, left, right)

    def add(i):
        swap(i).wait_recv()
        for c in range(2):
            get_partial(i, c).wait_recv()
        for sums, c in ((kept_ref, core), (twin_sum_ref, 1 - core)):
            mixed_ref[i, rows(c)] = (sums[i].astype(jnp.float32) + got_ref[i, rows(c)].astype(jnp.float32)).astype(
                jnp.bfloat16
            )

    for load in loads[:6] + loads[7:]:
        load.wait()

    def ready(rs, between):
        prepare(
            rs, between, q_ref, k_ref, v_ref, gate_ref, decay_ref, rate_ref, gain_ref, zhi_ref, zlo_ref, base_ref, gain_gate_ref
        )

    def merge_first():
        merge(0)
        for way in range(2):
            hop(way, requests - 1).start()
        merge(1)

    ready([0, 1], answer)
    ready([2, 3], merge_first)
    merge(2)
    merge(3)
    complete(0)
    complete(1)
    complete(2)
    for load in weight_loads:
        load.wait()
    for copy in got_weights:
        copy.wait_recv()
    project(0)
    complete(3)
    relay(0)
    project(1)
    relay(1)
    project(2)
    relay(2)
    project(3)
    relay(3)
    add(0)
    add(1)
    add(2)
    add(3)
    for i in range(requests):
        for way in range(2):
            pass_end(way, i).wait_recv()
    for target in range(requests):
        row = worker * requests + target
        mine, theirs = jnp.int32(0), jnp.int32(0)
        kept = jnp.bool_(False)
        for i in range(requests):
            here = slot_ref[i] == row
            kept = kept | here
            mine = jnp.where(here, i, mine)
            for n in range(4):
                theirs = jnp.where(told_smem[opposite(n), 0, 3 * requests + i] == row, n * requests + i, theirs)
        end_ref[target] = jnp.where(
            kept, sent_end_ref[mine], got_end_ref[theirs // requests, theirs % requests]
        )

    for copy in infos + weights:
        copy.wait_send()
    for i in range(requests):
        for way in range(2):
            hop(way, i).wait_send()
            lend(way, i).wait_send()
            send_end(way, i).wait_send()
            pass_end(way, i).wait_send()
        for kind in range(3):
            send_normed(kind, i).wait_send()
        for c in range(2):
            send_partial(i, c).wait_send()
        swap(i).wait_send()


def store_kernel(mixed_ref, end_ref, mixed_hbm, end_hbm, wide_ref, mixed_sem, end_sem):
    requests = mixed_ref.shape[0]
    copies = [pltpu.make_async_copy(mixed_ref.at[i], mixed_hbm.at[i], mixed_sem.at[i]) for i in range(requests)]
    for copy in copies:
        copy.start()
    for i in range(requests):
        wide_ref[i] = end_ref[i].astype(jnp.float32)
        copies.append(pltpu.make_async_copy(wide_ref.at[i], end_hbm.at[i], end_sem.at[i]))
        copies[-1].start()
    for copy in copies:
        copy.wait()


def on_device(
    queries,
    key_heads,
    values_in,
    out_gate,
    log_decay,
    write_rate,
    cache_states,
    norm_gain,
    out_proj,
    hit_owner,
    hit_node,
    prefix_len,
    write_slot,
):
    requests, tokens = queries.shape[:2]
    heads = log_decay.shape[1]
    width = heads * DV
    state = cache_states.shape[1:]
    vmem = pl.BlockSpec(memory_space=pltpu.VMEM)
    anywhere = pl.BlockSpec(memory_space=pltpu.HBM)
    low, wide = jnp.bfloat16, jnp.float32
    dma = pltpu.SemaphoreType.DMA
    mixed, ends = pl.pallas_call(
        functools.partial(layer_kernel, lax.axis_size("worker")),
        out_shape=(
            pltpu.VMEM((requests, tokens, width), low),
            pltpu.VMEM((requests, *state), low),
        ),
        in_specs=[anywhere] * 13,
        out_specs=(vmem, vmem),
        scratch_shapes=[
            *[pltpu.SMEM((requests,), jnp.int32)] * 4,
            pltpu.VMEM((1, DV), wide),
            pltpu.VMEM(queries.shape, low),
            pltpu.VMEM(key_heads.shape, low),
            pltpu.VMEM(values_in.shape, low),
            pltpu.VMEM(out_gate.shape, low),
            pltpu.VMEM(log_decay.shape, wide),
            pltpu.VMEM(write_rate.shape, wide),
            pltpu.VMEM(cache_states.shape, wide),
            pltpu.VMEM((requests * heads, tokens + DK, DK), low),
            pltpu.VMEM((requests * heads, tokens + DK, DK), low),
            pltpu.VMEM((requests * heads, tokens + DK, DV), wide),
            pltpu.VMEM((requests * heads, tokens, DV), wide),
            pltpu.VMEM((8, 128), jnp.int32),
            pltpu.VMEM((4, 8, 128), jnp.int32),
            pltpu.SMEM((4, 8, 128), jnp.int32),
            pltpu.VMEM((2, requests, *state), low),
            pltpu.VMEM((2, requests, *state), low),
            pltpu.VMEM((2, requests, *state), low),
            pltpu.VMEM((2, requests, *state), low),
            pltpu.VMEM((requests, *state), low),
            pltpu.VMEM((4, requests, *state), low),
            pltpu.VMEM((4, width, 4 * width), low),
            pltpu.VMEM((requests, tokens, width), low),
            pltpu.VMEM((requests, 3, tokens // 2, width), low),
            pltpu.VMEM((requests, tokens // 2, width), wide),
            pltpu.VMEM((requests, 2, tokens // 2, width), low),
            pltpu.VMEM((requests, tokens, width), low),
            pltpu.VMEM((requests, tokens // 2, width), low),
            pltpu.VMEM((requests, tokens // 2, width), low),
            dma((4,)),
            dma((8,)),
            dma((2,)),
            dma,
            dma((4,)),
            dma((4,)),
            dma((2, requests)),
            dma((2, requests)),
            dma((2, requests)),
            dma((2, requests)),
            dma((4, requests)),
            dma((4, requests)),
            dma((3, 2)),
            dma((3, 2)),
            dma((3, requests)),
            dma((3, requests)),
            dma((requests, 2)),
            dma((requests, 2)),
            dma((requests,)),
            dma((requests,)),
        ],
        compiler_params=pltpu.CompilerParams(
            collective_id=0, has_side_effects=True, vmem_limit_bytes=48 * 1024 * 1024
        ),
        name="layer",
    )(
        *(
            pltpu.with_memory_space_constraint(x, pltpu.HBM)
            for x in (
                hit_owner,
                hit_node,
                prefix_len,
                write_slot,
                norm_gain[None],
                queries,
                key_heads,
                values_in,
                out_gate,
                log_decay,
                write_rate,
                cache_states,
                out_proj,
            )
        )
    )
    return pl.pallas_call(
        store_kernel,
        out_shape=(jax.ShapeDtypeStruct(mixed.shape, low), jax.ShapeDtypeStruct(ends.shape, wide)),
        in_specs=[vmem] * 2,
        out_specs=(anywhere, anywhere),
        scratch_shapes=[pltpu.VMEM(ends.shape, wide), dma((requests,)), dma((requests,))],
        compiler_params=pltpu.CompilerParams(vmem_limit_bytes=32 * 1024 * 1024),
        name="store",
    )(mixed, ends)


def solution(mesh):
    in_specs = (
        P("worker", None, "tensor"),
        P("worker", None, "tensor"),
        P("worker", None, "tensor"),
        P("worker", None, "tensor"),
        P("worker", "tensor", None),
        P("worker", "tensor", None),
        P("worker", "tensor", None, None),
        P(),
        P("tensor", None),
        P("worker"),
        P("worker"),
        P("worker"),
        P("worker"),
    )
    out_specs = (P("worker", None, "tensor"), P("worker", "tensor", None, None))
    return jax.shard_map(
        on_device, mesh=mesh, in_specs=in_specs, out_specs=out_specs, check_vma=False
    )
```

```python
import functools

import jax
import jax.numpy as jnp
from jax import lax
from jax.experimental import pallas as pl
from jax.experimental.pallas import tpu as pltpu
from jax.sharding import PartitionSpec as P

DK = 128
DV = 128
REACH = 2
SMALL = 8
MESH = pl.DeviceIdType.MESH
OFFSETS = (-2, 2, -1, 1)
TWIN = 0


def split(x):
    hi = x.astype(jnp.bfloat16)
    return hi, (x - hi.astype(jnp.float32)).astype(jnp.bfloat16)


def dot1(a, b):
    return jnp.dot(a, b, preferred_element_type=jnp.float32)


def dot3(a, b):
    (a_hi, a_lo), (b_hi, b_lo) = a, b
    return dot1(jnp.concatenate([a_hi, a_lo, a_hi], axis=1), jnp.concatenate([b_hi, b_hi, b_lo], axis=0))


def dot_nt(a, b):
    return lax.dot_general(a, b, (((1,), (1,)), ((), ())), preferred_element_type=jnp.float32)


def dot_tn(a, b):
    return lax.dot_general(a, b, (((0,), (0,)), ((), ())), preferred_element_type=jnp.float32)


def iota(shape, dim):
    return lax.broadcasted_iota(jnp.int32, shape, dim)


def solve_small(compact):
    rows, lanes = compact.shape
    place = iota((rows, lanes), 1) % SMALL
    inverse = jnp.where(place == iota((rows, lanes), 0) % SMALL, 1.0, 0.0)
    for j in range(SMALL - 1):
        column = jnp.where(place == j, compact, 0.0)
        if j:
            column = pltpu.roll(column, lanes - j, 1)
        for step in (1, 2, 4):
            column = column + pltpu.roll(column, step, 1)
        groups = inverse.reshape(rows // SMALL, SMALL, lanes)
        row = jnp.broadcast_to(groups[:, j : j + 1, :], groups.shape).reshape(rows, lanes)
        inverse = inverse - column * row
    return inverse


def invert_unit_lower(systems):
    n = systems[0].shape[0]
    own = iota((n, n), 1) // SMALL == iota((n, n), 0) // SMALL
    compact = [
        jnp.sum(jnp.where(own, system, 0.0).reshape(n // SMALL, SMALL, n), axis=0) for system in systems
    ]
    small = solve_small(jnp.concatenate(compact, axis=0))
    inverses = []
    for i in range(len(systems)):
        block = small[i * SMALL : (i + 1) * SMALL]
        wide = jnp.broadcast_to(block[None], (n // SMALL, SMALL, n)).reshape(n, n)
        inverses.append(jnp.where(own, wide, 0.0))
    parts = [split(system) for system in systems]
    size = SMALL
    while size < n:
        row, lane = iota((n, n), 0) // size, iota((n, n), 1) // size
        below = (row % 2 == 1) & (row == lane + 1)
        cut = [tuple(jnp.where(below, part, jnp.zeros_like(part)) for part in pair) for pair in parts]
        halves = [split(inverse) for inverse in inverses]
        inner = [split(dot3(x, y)) for x, y in zip(cut, halves)]
        inverses = [inverse - dot3(x, y) for inverse, x, y in zip(inverses, halves, inner)]
        size *= 2
    return inverses


def prepare(
    rs, between, q_ref, k_ref, v_ref, gate_ref, decay_ref, rate_ref, gain_ref, zhi_ref, zlo_ref, base_ref, gain_gate_ref
):
    tokens = q_ref.shape[1]
    heads = decay_ref.shape[1]
    half = tokens // 2
    row, lane = iota((half, half), 0), iota((half, half), 1)
    upto = jnp.where(iota((tokens, tokens), 0) <= iota((tokens, tokens), 1), 1.0, 0.0).astype(jnp.bfloat16)
    decay = jnp.concatenate([decay_ref[r] for r in rs], axis=0)
    hi, _ = split(decay)
    rest = decay - hi.astype(jnp.float32)
    mid, low = split(rest)
    sums = dot1(jnp.concatenate([hi, mid, low], axis=0), upto)
    count = len(rs) * heads
    runnings = sums[2 * count :] + sums[count : 2 * count] + sums[:count]
    every = [runnings] + [rate_ref[r] for r in rs]
    pad = -2 * count % 8
    if pad:
        every.append(jnp.zeros((pad, tokens), jnp.float32))
    columns = jnp.concatenate(every, axis=0).T
    chains = []
    for n, r in enumerate(rs):
        q, k = q_ref[r], k_ref[r]
        qf, kf = q.astype(jnp.float32), k.astype(jnp.float32)
        rq = lax.rsqrt(jnp.sum(qf * qf, axis=1, keepdims=True) + 1e-06) * DK ** (-0.5)
        rk = lax.rsqrt(jnp.sum(kf * kf, axis=1, keepdims=True) + 1e-06)
        first, second = dot_nt(k, k[:half]), dot_nt(k[half:], k[half:])
        scales = [
            lax.rsqrt(jnp.sum(jnp.where(row == lane, raw, 0.0), axis=0, keepdims=True) + 1e-06)
            for raw in (first[:half], second)
        ]
        kk = [
            first[:half] * (scales[0] * rk[:half]),
            first[half:] * (scales[0] * rk[half:]),
            second * (scales[1] * rk[half:]),
        ]
        first, second = dot_nt(q, k[:half]), dot_nt(q[half:], k[half:])
        qk = [
            first[:half] * (scales[0] * rq[:half]),
            first[half:] * (scales[0] * rq[half:]),
            second * (scales[1] * rq[half:]),
        ]
        for h in range(heads):
            c = n * heads + h
            chains.append((r, h, qf, kf, rq, rk, kk, qk, columns[:, c : c + 1], columns[:, count + c : count + c + 1], runnings[c : c + 1]))
    systems, crosses, reads = [], [], []
    for r, h, qf, kf, rq, rk, kk, qk, g, rate, ahead in chains:
        within = [
            jnp.exp(jnp.where(row >= lane, g[:half] - ahead[:, :half], -jnp.inf)),
            jnp.exp(g[half:] - ahead[:, :half]),
            jnp.exp(jnp.where(row >= lane, g[half:] - ahead[:, half:], -jnp.inf)),
        ]
        systems.append(jnp.where(row > lane, rate[:half] * (within[0] * kk[0]), 0.0))
        systems.append(jnp.where(row > lane, rate[half:] * (within[2] * kk[2]), 0.0))
        crosses.append(split(rate[half:] * (within[1] * kk[1])))
        reads.append([split(x * y) for x, y in zip(within, qk)])
    inverses = [split(x) for x in invert_unit_lower(systems)]
    between()
    rights = []
    for r, h, qf, kf, rq, rk, kk, qk, g, rate, ahead in chains:
        values = v_ref[r, :, h * DV : (h + 1) * DV].astype(jnp.float32)
        rights.append(jnp.concatenate([rate * values, (rate * jnp.exp(g) * rk) * kf], axis=1))
    tops = [split(dot3(x, split(y[:half]))) for x, y in zip(inverses[::2], rights)]
    rests = [y[half:] - dot3(x, top) for x, y, top in zip(crosses, rights, tops)]
    bottoms = [split(dot3(x, split(rest))) for x, rest in zip(inverses[1::2], rests)]
    solveds = [
        tuple(jnp.concatenate([x, y], axis=0) for x, y in zip(top, bottom)) for top, bottom in zip(tops, bottoms)
    ]
    read_tops = [dot3(read[0], top) for read, top in zip(reads, tops)]
    read_bottoms = [
        dot3(tuple(jnp.concatenate([x, y], axis=1) for x, y in zip(read[1], read[2])), solved)
        for read, solved in zip(reads, solveds)
    ]
    ends = []
    for (r, h, qf, kf, rq, rk, kk, qk, g, rate, ahead), solved in zip(chains, solveds):
        hi, lo = split((jnp.exp(g[tokens - 1 :] - g) * rk) * kf)
        ends.append(dot_tn(jnp.concatenate([hi, lo, hi], axis=0), jnp.concatenate([solved[0], solved[0], solved[1]], axis=0)))
    eye = iota((DK, DK), 0) == iota((DK, DK), 1)
    for (r, h, qf, kf, rq, rk, kk, qk, g, rate, ahead), top, bottom, end in zip(chains, read_tops, read_bottoms, ends):
        slot = r * heads + h
        base_ref[slot, :half] = top[:, :DV]
        base_ref[slot, half:tokens] = bottom[:, :DV]
        base_ref[slot, tokens:] = end[:, :DV]
        from_state = (jnp.exp(g) * rq) * qf - jnp.concatenate([top[:, DV:], bottom[:, DV:]], axis=0)
        to_state = jnp.where(eye, jnp.exp(g[tokens - 1 :]), 0.0) - end[:, DV:]
        z_hi, z_lo = split(jnp.concatenate([from_state, to_state], axis=0))
        zhi_ref[slot] = z_hi
        zlo_ref[slot] = z_lo
        gate = gate_ref[r, :, h * DV : (h + 1) * DV].astype(jnp.float32)
        gain_gate_ref[slot] = gain_ref[...] * (gate / (1.0 + jnp.exp(-gate)))


def finish(slots, starts, zhi_ref, zlo_ref, base_ref, gain_gate_ref):
    tokens = gain_gate_ref.shape[1]
    wholes = [
        dot1(zhi_ref[slot], start) + dot1(zlo_ref[slot], start) + base_ref[slot] for slot, start in zip(slots, starts)
    ]
    scales = [
        lax.rsqrt(jnp.mean(whole[:tokens] * whole[:tokens], axis=1, keepdims=True) + 1e-06) for whole in wholes
    ]
    normed = [
        (whole[:tokens] * scale * gain_gate_ref[slot]).astype(jnp.bfloat16)
        for slot, whole, scale in zip(slots, wholes, scales)
    ]
    return normed, [whole[tokens:] for whole in wholes]


def layer_kernel(
    workers,
    owner_hbm,
    node_hbm,
    prefix_hbm,
    slot_hbm,
    gain_hbm,
    q_hbm,
    k_hbm,
    v_hbm,
    gate_hbm,
    decay_hbm,
    rate_hbm,
    cache_hbm,
    proj_hbm,
    mixed_ref,
    end_ref,
    owner_ref,
    node_ref,
    prefix_ref,
    slot_ref,
    gain_ref,
    q_ref,
    k_ref,
    v_ref,
    gate_ref,
    decay_ref,
    rate_ref,
    cache_ref,
    zhi_ref,
    zlo_ref,
    base_ref,
    gain_gate_ref,
    info_ref,
    told_ref,
    told_smem,
    hop_out_ref,
    hop_in_ref,
    lent_ref,
    borrowed_ref,
    sent_end_ref,
    got_end_ref,
    weight_ref,
    normed_ref,
    gathered_ref,
    kept_ref,
    passed_ref,
    got_ref,
    lent_sum_ref,
    twin_sum_ref,
    ask_sem,
    load_sem,
    weight_load_sem,
    told_sem,
    info_send,
    info_recv,
    hop_send,
    hop_recv,
    lend_send,
    lend_recv,
    end_send,
    end_recv,
    weight_send,
    weight_recv,
    normed_send,
    normed_recv,
    partial_send,
    partial_recv,
    swap_send,
    swap_recv,
):
    requests, tokens = q_ref.shape[:2]
    half = tokens // 2
    heads = decay_ref.shape[1]
    width = heads * DV
    slots = cache_ref.shape[0]
    worker = lax.axis_index("worker")
    tensor = lax.axis_index("tensor")
    chip, core = tensor // 2, tensor % 2

    def paired(there, way):
        return (1 - way) * (there + 1 - 2 * (there % 2)) + way * (3 - there)

    near = [(lax.rem(worker + workers + o, workers), tensor) for o in OFFSETS]
    twin = 2 * chip + 1 - core
    others = [twin] + [2 * paired(chip, way) + c for way in range(2) for c in range(2)]
    beyond = paired(chip, 1 - core)

    def remote(src, dst, send, recv, device):
        return pltpu.make_async_remote_copy(
            src_ref=src, dst_ref=dst, send_sem=send, recv_sem=recv, device_id=device, device_id_type=MESH
        )

    barrier = pltpu.get_barrier_semaphore()
    for device in near + [(worker, index) for index in others]:
        pl.semaphore_signal(barrier, inc=1, device_id=device, device_id_type=MESH)
    asks = [
        pltpu.make_async_copy(src, dst, ask_sem.at[i])
        for i, (src, dst) in enumerate(
            ((owner_hbm, owner_ref), (node_hbm, node_ref), (prefix_hbm, prefix_ref), (slot_hbm, slot_ref))
        )
    ]
    for ask in asks:
        ask.start()
    loads = [
        pltpu.make_async_copy(src, dst, load_sem.at[i])
        for i, (src, dst) in enumerate(
            (
                (q_hbm, q_ref),
                (k_hbm, k_ref),
                (v_hbm, v_ref),
                (decay_hbm, decay_ref),
                (rate_hbm, rate_ref),
                (gate_hbm, gate_ref),
                (cache_hbm, cache_ref),
                (gain_hbm, gain_ref),
            )
        )
    ]
    for load in loads:
        load.start()

    def columns(there):
        return pl.ds(pl.multiple_of(there * 2 * width, 2 * width), 2 * width)

    def rows(c):
        return pl.ds(pl.multiple_of(c * half, half), half)

    weight_loads = [
        pltpu.make_async_copy(
            proj_hbm.at[:, columns(there)],
            weight_ref.at[0, :, pl.ds(part * 2 * width, 2 * width)],
            weight_load_sem.at[part],
        )
        for part, there in enumerate((chip, beyond))
    ]
    for load in weight_loads:
        load.start()

    for ask in asks:
        ask.wait()
    lane = iota((8, 128), 1)
    block = jnp.zeros((8, 128), jnp.int32)
    for part, ref in enumerate((owner_ref, node_ref, prefix_ref, slot_ref)):
        for i in range(requests):
            block = jnp.where(lane == part * requests + i, ref[i], block)
    info_ref[...] = block

    pl.semaphore_wait(barrier, len(near) + len(others))

    def opposite(n):
        return n ^ 1

    infos = [
        remote(info_ref, told_ref.at[opposite(n)], info_send.at[n], info_recv.at[opposite(n)], near[n])
        for n in range(4)
    ]
    for copy in infos:
        copy.start()

    def route(kind):
        if kind == TWIN:
            return twin, 1, 1 - core, chip
        way = kind - 1
        there = paired(chip, way)
        return 2 * there + way, 2 + lax.rem(core + way, 2), way, there

    weights = []
    for kind in (1, 2, TWIN):
        index, source, way, there = route(kind)
        for part, block in enumerate((there, paired(there, 1 - way))):
            weights.append(
                remote(
                    proj_hbm.at[:, columns(block)],
                    weight_ref.at[source, :, pl.ds(part * 2 * width, 2 * width)],
                    weight_send.at[kind, part],
                    weight_recv.at[source - 1, part],
                    (worker, index),
                )
            )
    got_weights = [
        remote(
            proj_hbm.at[:, columns(chip)],
            weight_ref.at[source, :, pl.ds(part * 2 * width, 2 * width)],
            weight_send.at[source - 1, part],
            weight_recv.at[source - 1, part],
            (worker, twin),
        )
        for source in range(1, 4)
        for part in range(2)
    ]
    for copy in weights:
        copy.start()

    def hop(way, i):
        return remote(
            hop_out_ref.at[way, i], hop_in_ref.at[way, i], hop_send.at[way, i], hop_recv.at[way, i], near[2 + way]
        )

    def lend(way, i):
        return remote(
            lent_ref.at[way, i], borrowed_ref.at[way, i], lend_send.at[way, i], lend_recv.at[way, i], near[2 + way]
        )

    def send_end(way, i):
        return remote(
            sent_end_ref.at[i], got_end_ref.at[2 + way, i], end_send.at[2 + way, i], end_recv.at[2 + way, i], near[2 + way]
        )

    def pass_end(way, i):
        return remote(
            got_end_ref.at[2 + way, i], got_end_ref.at[way, i], end_send.at[way, i], end_recv.at[way, i], near[2 + way]
        )

    def send_normed(kind, i):
        index, source, way, _ = route(kind)
        return remote(
            normed_ref.at[i, rows(way)],
            gathered_ref.at[i, source - 1],
            normed_send.at[kind, i],
            normed_recv.at[source - 1, i],
            (worker, index),
        )

    def get_normed(source, i):
        return remote(
            normed_ref.at[i, rows(core)],
            gathered_ref.at[i, source - 1],
            normed_send.at[source - 1, i],
            normed_recv.at[source - 1, i],
            (worker, twin),
        )

    def send_partial(i, c):
        return remote(
            passed_ref.at[i, c],
            got_ref.at[i, rows(core)],
            partial_send.at[i, c],
            partial_recv.at[i, core],
            (worker, 2 * beyond + c),
        )

    def get_partial(i, c):
        return remote(
            passed_ref.at[i, c], got_ref.at[i, rows(c)], partial_send.at[i, c], partial_recv.at[i, c], (worker, twin)
        )

    def swap(i):
        return remote(lent_sum_ref.at[i], twin_sum_ref.at[i], swap_send.at[i], swap_recv.at[i], (worker, twin))

    def wanted(n, i):
        return cache_ref[jnp.clip(told_smem[n, 0, requests + i], 0, slots - 1)].astype(jnp.bfloat16)

    def answer():
        for n in range(4):
            remote(info_ref, told_ref.at[n], info_send.at[n], info_recv.at[n], near[n]).wait_recv()
        fetch = pltpu.make_async_copy(told_ref, told_smem, told_sem)
        fetch.start()
        fetch.wait()
        loads[6].wait()
        @pl.loop(0, requests)
        def _(i):
            for way in range(2):
                hop_out_ref[way, i] = wanted(way, i)
                hop(way, i).start()

    def merge(i):
        for way in range(2):
            hop(way, i).wait_recv()
            mine = told_smem[2 + way, 0, i] == worker
            lent_ref[way, i] = jnp.where(mine, wanted(2 + way, i), hop_in_ref[way, i])
            lend(way, i).start()

    def complete(i):
        for way in range(2):
            lend(way, i).wait_recv()
        move = lax.rem(owner_ref[i] - worker + workers + REACH, workers) - REACH
        node = jnp.clip(node_ref[i], 0, slots - 1)
        cached = prefix_ref[i] > 0
        starts = []
        for h in range(heads):
            start = cache_ref[node, h].astype(jnp.bfloat16)
            start = jnp.where(move < 0, borrowed_ref[1, i, h], start)
            start = jnp.where(move > 0, borrowed_ref[0, i, h], start)
            starts.append(jnp.where(cached, start, jnp.zeros_like(start)))
        slots_here = [i * heads + h for h in range(heads)]
        normed, ends = finish(slots_here, starts, zhi_ref, zlo_ref, base_ref, gain_gate_ref)
        for h in range(heads):
            normed_ref[i, :, h * DV : (h + 1) * DV] = normed[h]
            sent_end_ref[i, h] = ends[h].astype(jnp.bfloat16)
        for kind in (1, 2, TWIN):
            send_normed(kind, i).start()
        for way in range(2):
            send_end(way, i).start()

    def relay(i):
        for way in range(2):
            send_end(way, i).wait_recv()
            pass_end(way, i).start()

    def project(i):
        total = dot1(normed_ref[i, rows(core)], weight_ref[0])
        for source in range(1, 4):
            get_normed(source, i).wait_recv()
            total = total + dot1(gathered_ref[i, source - 1], weight_ref[source])
        for c in range(2):
            passed_ref[i, c] = total[:, (2 + c) * width : (3 + c) * width].astype(jnp.bfloat16)
            send_partial(i, c).start()
        left, right = total[:, :width], total[:, width : 2 * width]
        lent_sum_ref[i] = jnp.where(core == 0, right, left).astype(jnp.bfloat16)
        swap(i).start()
        kept_ref[i] = jnp.where(core == 0, left, right)

    def add(i):
        swap(i).wait_recv()
        for c in range(2):
            get_partial(i, c).wait_recv()
        for sums, c in ((kept_ref, core), (twin_sum_ref, 1 - core)):
            mixed_ref[i, rows(c)] = (sums[i].astype(jnp.float32) + got_ref[i, rows(c)].astype(jnp.float32)).astype(
                jnp.bfloat16
            )

    for load in loads[:6] + loads[7:]:
        load.wait()

    def ready(rs, between):
        prepare(
            rs, between, q_ref, k_ref, v_ref, gate_ref, decay_ref, rate_ref, gain_ref, zhi_ref, zlo_ref, base_ref, gain_gate_ref
        )

    def merge_first():
        pl.loop(0, 2)(merge)

    ready([0, 1], answer)
    ready([2, 3], merge_first)
    pl.loop(2, requests)(merge)
    pl.loop(0, requests)(complete)
    for load in weight_loads:
        load.wait()
    for copy in got_weights:
        copy.wait_recv()

    @pl.loop(0, requests)
    def _(i):
        project(i)
        relay(i)

    pl.loop(0, requests)(add)
    for i in range(requests):
        for way in range(2):
            pass_end(way, i).wait_recv()
    for target in range(requests):
        row = worker * requests + target
        mine, theirs = jnp.int32(0), jnp.int32(0)
        kept = jnp.bool_(False)
        for i in range(requests):
            here = slot_ref[i] == row
            kept = kept | here
            mine = jnp.where(here, i, mine)
            for n in range(4):
                theirs = jnp.where(told_smem[opposite(n), 0, 3 * requests + i] == row, n * requests + i, theirs)
        end_ref[target] = jnp.where(
            kept, sent_end_ref[mine], got_end_ref[theirs // requests, theirs % requests]
        )

    for copy in infos + weights:
        copy.wait_send()
    for i in range(requests):
        for way in range(2):
            hop(way, i).wait_send()
            lend(way, i).wait_send()
            send_end(way, i).wait_send()
            pass_end(way, i).wait_send()
        for kind in range(3):
            send_normed(kind, i).wait_send()
        for c in range(2):
            send_partial(i, c).wait_send()
        swap(i).wait_send()


def store_kernel(mixed_ref, end_ref, mixed_hbm, end_hbm, wide_ref, mixed_sem, end_sem):
    requests = mixed_ref.shape[0]
    copies = [pltpu.make_async_copy(mixed_ref.at[i], mixed_hbm.at[i], mixed_sem.at[i]) for i in range(requests)]
    for copy in copies:
        copy.start()
    for i in range(requests):
        wide_ref[i] = end_ref[i].astype(jnp.float32)
        copies.append(pltpu.make_async_copy(wide_ref.at[i], end_hbm.at[i], end_sem.at[i]))
        copies[-1].start()
    for copy in copies:
        copy.wait()


def on_device(
    queries,
    key_heads,
    values_in,
    out_gate,
    log_decay,
    write_rate,
    cache_states,
    norm_gain,
    out_proj,
    hit_owner,
    hit_node,
    prefix_len,
    write_slot,
):
    requests, tokens = queries.shape[:2]
    heads = log_decay.shape[1]
    width = heads * DV
    state = cache_states.shape[1:]
    vmem = pl.BlockSpec(memory_space=pltpu.VMEM)
    anywhere = pl.BlockSpec(memory_space=pltpu.HBM)
    low, wide = jnp.bfloat16, jnp.float32
    dma = pltpu.SemaphoreType.DMA
    mixed, ends = pl.pallas_call(
        functools.partial(layer_kernel, lax.axis_size("worker")),
        out_shape=(
            pltpu.VMEM((requests, tokens, width), low),
            pltpu.VMEM((requests, *state), low),
        ),
        in_specs=[anywhere] * 13,
        out_specs=(vmem, vmem),
        scratch_shapes=[
            *[pltpu.SMEM((requests,), jnp.int32)] * 4,
            pltpu.VMEM((1, DV), wide),
            pltpu.VMEM(queries.shape, low),
            pltpu.VMEM(key_heads.shape, low),
            pltpu.VMEM(values_in.shape, low),
            pltpu.VMEM(out_gate.shape, low),
            pltpu.VMEM(log_decay.shape, wide),
            pltpu.VMEM(write_rate.shape, wide),
            pltpu.VMEM(cache_states.shape, wide),
            pltpu.VMEM((requests * heads, tokens + DK, DK), low),
            pltpu.VMEM((requests * heads, tokens + DK, DK), low),
            pltpu.VMEM((requests * heads, tokens + DK, DV), wide),
            pltpu.VMEM((requests * heads, tokens, DV), wide),
            pltpu.VMEM((8, 128), jnp.int32),
            pltpu.VMEM((4, 8, 128), jnp.int32),
            pltpu.SMEM((4, 8, 128), jnp.int32),
            pltpu.VMEM((2, requests, *state), low),
            pltpu.VMEM((2, requests, *state), low),
            pltpu.VMEM((2, requests, *state), low),
            pltpu.VMEM((2, requests, *state), low),
            pltpu.VMEM((requests, *state), low),
            pltpu.VMEM((4, requests, *state), low),
            pltpu.VMEM((4, width, 4 * width), low),
            pltpu.VMEM((requests, tokens, width), low),
            pltpu.VMEM((requests, 3, tokens // 2, width), low),
            pltpu.VMEM((requests, tokens // 2, width), wide),
            pltpu.VMEM((requests, 2, tokens // 2, width), low),
            pltpu.VMEM((requests, tokens, width), low),
            pltpu.VMEM((requests, tokens // 2, width), low),
            pltpu.VMEM((requests, tokens // 2, width), low),
            dma((4,)),
            dma((8,)),
            dma((2,)),
            dma,
            dma((4,)),
            dma((4,)),
            dma((2, requests)),
            dma((2, requests)),
            dma((2, requests)),
            dma((2, requests)),
            dma((4, requests)),
            dma((4, requests)),
            dma((3, 2)),
            dma((3, 2)),
            dma((3, requests)),
            dma((3, requests)),
            dma((requests, 2)),
            dma((requests, 2)),
            dma((requests,)),
            dma((requests,)),
        ],
        compiler_params=pltpu.CompilerParams(
            collective_id=0, has_side_effects=True, vmem_limit_bytes=48 * 1024 * 1024
        ),
        name="layer",
    )(
        *(
            pltpu.with_memory_space_constraint(x, pltpu.HBM)
            for x in (
                hit_owner,
                hit_node,
                prefix_len,
                write_slot,
                norm_gain[None],
                queries,
                key_heads,
                values_in,
                out_gate,
                log_decay,
                write_rate,
                cache_states,
                out_proj,
            )
        )
    )
    return pl.pallas_call(
        store_kernel,
        out_shape=(jax.ShapeDtypeStruct(mixed.shape, low), jax.ShapeDtypeStruct(ends.shape, wide)),
        in_specs=[vmem] * 2,
        out_specs=(anywhere, anywhere),
        scratch_shapes=[pltpu.VMEM(ends.shape, wide), dma((requests,)), dma((requests,))],
        compiler_params=pltpu.CompilerParams(vmem_limit_bytes=32 * 1024 * 1024),
        name="store",
    )(mixed, ends)


def solution(mesh):
    in_specs = (
        P("worker", None, "tensor"),
        P("worker", None, "tensor"),
        P("worker", None, "tensor"),
        P("worker", None, "tensor"),
        P("worker", "tensor", None),
        P("worker", "tensor", None),
        P("worker", "tensor", None, None),
        P(),
        P("tensor", None),
        P("worker"),
        P("worker"),
        P("worker"),
        P("worker"),
    )
    out_specs = (P("worker", None, "tensor"), P("worker", "tensor", None, None))
    return jax.shard_map(
        on_device, mesh=mesh, in_specs=in_specs, out_specs=out_specs, check_vma=False
    )
```

```python
import functools

import jax
import jax.numpy as jnp
from jax import lax
from jax.experimental import pallas as pl
from jax.experimental.pallas import tpu as pltpu
from jax.sharding import PartitionSpec as P

DK = 128
DV = 128
REACH = 2
SMALL = 8
MESH = pl.DeviceIdType.MESH
OFFSETS = (-2, 2, -1, 1)
TWIN = 0


def split(x):
    hi = x.astype(jnp.bfloat16)
    return hi, (x - hi.astype(jnp.float32)).astype(jnp.bfloat16)


def dot1(a, b):
    return jnp.dot(a, b, preferred_element_type=jnp.float32)


def dot3(a, b):
    (a_hi, a_lo), (b_hi, b_lo) = a, b
    return dot1(jnp.concatenate([a_hi, a_lo, a_hi], axis=1), jnp.concatenate([b_hi, b_hi, b_lo], axis=0))


def dot_nt(a, b):
    return lax.dot_general(a, b, (((1,), (1,)), ((), ())), preferred_element_type=jnp.float32)


def dot_tn(a, b):
    return lax.dot_general(a, b, (((0,), (0,)), ((), ())), preferred_element_type=jnp.float32)


def iota(shape, dim):
    return lax.broadcasted_iota(jnp.int32, shape, dim)


def solve_small(compact):
    rows, lanes = compact.shape
    place = iota((rows, lanes), 1) % SMALL
    inverse = jnp.where(place == iota((rows, lanes), 0) % SMALL, 1.0, 0.0)
    for j in range(SMALL - 1):
        column = jnp.where(place == j, compact, 0.0)
        if j:
            column = pltpu.roll(column, lanes - j, 1)
        for step in (1, 2, 4):
            column = column + pltpu.roll(column, step, 1)
        groups = inverse.reshape(rows // SMALL, SMALL, lanes)
        row = jnp.broadcast_to(groups[:, j : j + 1, :], groups.shape).reshape(rows, lanes)
        inverse = inverse - column * row
    return inverse


def invert_unit_lower(systems):
    n = systems[0].shape[0]
    own = iota((n, n), 1) // SMALL == iota((n, n), 0) // SMALL
    compact = [
        jnp.sum(jnp.where(own, system, 0.0).reshape(n // SMALL, SMALL, n), axis=0) for system in systems
    ]
    small = solve_small(jnp.concatenate(compact, axis=0))
    inverses = []
    for i in range(len(systems)):
        block = small[i * SMALL : (i + 1) * SMALL]
        wide = jnp.broadcast_to(block[None], (n // SMALL, SMALL, n)).reshape(n, n)
        inverses.append(jnp.where(own, wide, 0.0))
    parts = [split(system) for system in systems]
    size = SMALL
    while size < n:
        row, lane = iota((n, n), 0) // size, iota((n, n), 1) // size
        below = (row % 2 == 1) & (row == lane + 1)
        cut = [tuple(jnp.where(below, part, jnp.zeros_like(part)) for part in pair) for pair in parts]
        halves = [split(inverse) for inverse in inverses]
        inner = [split(dot3(x, y)) for x, y in zip(cut, halves)]
        inverses = [inverse - dot3(x, y) for inverse, x, y in zip(inverses, halves, inner)]
        size *= 2
    return inverses


def prepare(
    rs, between, q_ref, k_ref, v_ref, gate_ref, decay_ref, rate_ref, gain_ref, zhi_ref, zlo_ref, base_ref, gain_gate_ref
):
    tokens = q_ref.shape[1]
    heads = decay_ref.shape[1]
    half = tokens // 2
    row, lane = iota((half, half), 0), iota((half, half), 1)
    upto = jnp.where(iota((tokens, tokens), 0) <= iota((tokens, tokens), 1), 1.0, 0.0).astype(jnp.bfloat16)
    decay = jnp.concatenate([decay_ref[r] for r in rs], axis=0)
    hi, _ = split(decay)
    rest = decay - hi.astype(jnp.float32)
    mid, low = split(rest)
    sums = dot1(jnp.concatenate([hi, mid, low], axis=0), upto)
    count = len(rs) * heads
    runnings = sums[2 * count :] + sums[count : 2 * count] + sums[:count]
    every = [runnings] + [rate_ref[r] for r in rs]
    pad = -2 * count % 8
    if pad:
        every.append(jnp.zeros((pad, tokens), jnp.float32))
    columns = jnp.concatenate(every, axis=0).T
    chains = []
    for n, r in enumerate(rs):
        q, k = q_ref[r], k_ref[r]
        qf, kf = q.astype(jnp.float32), k.astype(jnp.float32)
        rq = lax.rsqrt(jnp.sum(qf * qf, axis=1, keepdims=True) + 1e-06) * DK ** (-0.5)
        rk = lax.rsqrt(jnp.sum(kf * kf, axis=1, keepdims=True) + 1e-06)
        first, second = dot_nt(k, k[:half]), dot_nt(k[half:], k[half:])
        scales = [
            lax.rsqrt(jnp.sum(jnp.where(row == lane, raw, 0.0), axis=0, keepdims=True) + 1e-06)
            for raw in (first[:half], second)
        ]
        kk = [
            first[:half] * (scales[0] * rk[:half]),
            first[half:] * (scales[0] * rk[half:]),
            second * (scales[1] * rk[half:]),
        ]
        first, second = dot_nt(q, k[:half]), dot_nt(q[half:], k[half:])
        qk = [
            first[:half] * (scales[0] * rq[:half]),
            first[half:] * (scales[0] * rq[half:]),
            second * (scales[1] * rq[half:]),
        ]
        for h in range(heads):
            c = n * heads + h
            chains.append((r, h, qf, kf, rq, rk, kk, qk, columns[:, c : c + 1], columns[:, count + c : count + c + 1], runnings[c : c + 1]))
    systems, crosses, reads = [], [], []
    for r, h, qf, kf, rq, rk, kk, qk, g, rate, ahead in chains:
        within = [
            jnp.exp(jnp.where(row >= lane, g[:half] - ahead[:, :half], -jnp.inf)),
            jnp.exp(g[half:] - ahead[:, :half]),
            jnp.exp(jnp.where(row >= lane, g[half:] - ahead[:, half:], -jnp.inf)),
        ]
        systems.append(jnp.where(row > lane, rate[:half] * (within[0] * kk[0]), 0.0))
        systems.append(jnp.where(row > lane, rate[half:] * (within[2] * kk[2]), 0.0))
        crosses.append(split(rate[half:] * (within[1] * kk[1])))
        reads.append([split(x * y) for x, y in zip(within, qk)])
    inverses = [split(x) for x in invert_unit_lower(systems)]
    between()
    rights = []
    for r, h, qf, kf, rq, rk, kk, qk, g, rate, ahead in chains:
        values = v_ref[r, :, h * DV : (h + 1) * DV].astype(jnp.float32)
        rights.append(jnp.concatenate([rate * values, (rate * jnp.exp(g) * rk) * kf], axis=1))
    tops = [split(dot3(x, split(y[:half]))) for x, y in zip(inverses[::2], rights)]
    rests = [y[half:] - dot3(x, top) for x, y, top in zip(crosses, rights, tops)]
    bottoms = [split(dot3(x, split(rest))) for x, rest in zip(inverses[1::2], rests)]
    solveds = [
        tuple(jnp.concatenate([x, y], axis=0) for x, y in zip(top, bottom)) for top, bottom in zip(tops, bottoms)
    ]
    read_tops = [dot3(read[0], top) for read, top in zip(reads, tops)]
    read_bottoms = [
        dot3(tuple(jnp.concatenate([x, y], axis=1) for x, y in zip(read[1], read[2])), solved)
        for read, solved in zip(reads, solveds)
    ]
    ends = []
    for (r, h, qf, kf, rq, rk, kk, qk, g, rate, ahead), solved in zip(chains, solveds):
        hi, lo = split((jnp.exp(g[tokens - 1 :] - g) * rk) * kf)
        ends.append(dot_tn(jnp.concatenate([hi, lo, hi], axis=0), jnp.concatenate([solved[0], solved[0], solved[1]], axis=0)))
    eye = iota((DK, DK), 0) == iota((DK, DK), 1)
    for (r, h, qf, kf, rq, rk, kk, qk, g, rate, ahead), top, bottom, end in zip(chains, read_tops, read_bottoms, ends):
        slot = r * heads + h
        base_ref[slot, :half] = top[:, :DV]
        base_ref[slot, half:tokens] = bottom[:, :DV]
        base_ref[slot, tokens:] = end[:, :DV]
        from_state = (jnp.exp(g) * rq) * qf - jnp.concatenate([top[:, DV:], bottom[:, DV:]], axis=0)
        to_state = jnp.where(eye, jnp.exp(g[tokens - 1 :]), 0.0) - end[:, DV:]
        z_hi, z_lo = split(jnp.concatenate([from_state, to_state], axis=0))
        zhi_ref[slot] = z_hi
        zlo_ref[slot] = z_lo
        gate = gate_ref[r, :, h * DV : (h + 1) * DV].astype(jnp.float32)
        gain_gate_ref[slot] = gain_ref[...] * (gate / (1.0 + jnp.exp(-gate)))


def finish(slots, starts, zhi_ref, zlo_ref, base_ref, gain_gate_ref):
    tokens = gain_gate_ref.shape[1]
    wholes = [
        dot1(zhi_ref[slot], start) + dot1(zlo_ref[slot], start) + base_ref[slot] for slot, start in zip(slots, starts)
    ]
    scales = [
        lax.rsqrt(jnp.mean(whole[:tokens] * whole[:tokens], axis=1, keepdims=True) + 1e-06) for whole in wholes
    ]
    normed = [
        (whole[:tokens] * scale * gain_gate_ref[slot]).astype(jnp.bfloat16)
        for slot, whole, scale in zip(slots, wholes, scales)
    ]
    return normed, [whole[tokens:] for whole in wholes]


def layer_kernel(
    workers,
    owner_hbm,
    node_hbm,
    prefix_hbm,
    slot_hbm,
    gain_hbm,
    q_hbm,
    k_hbm,
    v_hbm,
    gate_hbm,
    decay_hbm,
    rate_hbm,
    cache_hbm,
    proj_hbm,
    mixed_ref,
    end_ref,
    owner_ref,
    node_ref,
    prefix_ref,
    slot_ref,
    gain_ref,
    q_ref,
    k_ref,
    v_ref,
    gate_ref,
    decay_ref,
    rate_ref,
    cache_ref,
    zhi_ref,
    zlo_ref,
    base_ref,
    gain_gate_ref,
    info_ref,
    told_ref,
    told_smem,
    hop_out_ref,
    hop_in_ref,
    lent_ref,
    borrowed_ref,
    sent_end_ref,
    got_end_ref,
    weight_ref,
    normed_ref,
    gathered_ref,
    kept_ref,
    passed_ref,
    got_ref,
    lent_sum_ref,
    twin_sum_ref,
    ask_sem,
    load_sem,
    weight_load_sem,
    told_sem,
    info_send,
    info_recv,
    hop_send,
    hop_recv,
    lend_send,
    lend_recv,
    end_send,
    end_recv,
    weight_send,
    weight_recv,
    normed_send,
    normed_recv,
    partial_send,
    partial_recv,
    swap_send,
    swap_recv,
):
    requests, tokens = q_ref.shape[:2]
    half = tokens // 2
    heads = decay_ref.shape[1]
    width = heads * DV
    slots = cache_ref.shape[0]
    worker = lax.axis_index("worker")
    tensor = lax.axis_index("tensor")
    chip, core = tensor // 2, tensor % 2

    def paired(there, way):
        return (1 - way) * (there + 1 - 2 * (there % 2)) + way * (3 - there)

    near = [(lax.rem(worker + workers + o, workers), tensor) for o in OFFSETS]
    twin = 2 * chip + 1 - core
    others = [twin] + [2 * paired(chip, way) + c for way in range(2) for c in range(2)]
    beyond = paired(chip, 1 - core)

    def remote(src, dst, send, recv, device):
        return pltpu.make_async_remote_copy(
            src_ref=src, dst_ref=dst, send_sem=send, recv_sem=recv, device_id=device, device_id_type=MESH
        )

    barrier = pltpu.get_barrier_semaphore()
    for device in near + [(worker, index) for index in others]:
        pl.semaphore_signal(barrier, inc=1, device_id=device, device_id_type=MESH)
    asks = [
        pltpu.make_async_copy(src, dst, ask_sem.at[i])
        for i, (src, dst) in enumerate(
            ((owner_hbm, owner_ref), (node_hbm, node_ref), (prefix_hbm, prefix_ref), (slot_hbm, slot_ref))
        )
    ]
    for ask in asks:
        ask.start()
    loads = [
        pltpu.make_async_copy(src, dst, load_sem.at[i])
        for i, (src, dst) in enumerate(
            (
                (q_hbm, q_ref),
                (k_hbm, k_ref),
                (v_hbm, v_ref),
                (decay_hbm, decay_ref),
                (rate_hbm, rate_ref),
                (gate_hbm, gate_ref),
                (cache_hbm, cache_ref),
                (gain_hbm, gain_ref),
            )
        )
    ]
    for load in loads:
        load.start()

    def columns(there):
        return pl.ds(pl.multiple_of(there * 2 * width, 2 * width), 2 * width)

    def rows(c):
        return pl.ds(pl.multiple_of(c * half, half), half)

    weight_loads = [
        pltpu.make_async_copy(
            proj_hbm.at[:, columns(there)],
            weight_ref.at[0, :, pl.ds(part * 2 * width, 2 * width)],
            weight_load_sem.at[part],
        )
        for part, there in enumerate((chip, beyond))
    ]
    for load in weight_loads:
        load.start()

    for ask in asks:
        ask.wait()
    lane = iota((8, 128), 1)
    block = jnp.zeros((8, 128), jnp.int32)
    for part, ref in enumerate((owner_ref, node_ref, prefix_ref, slot_ref)):
        for i in range(requests):
            block = jnp.where(lane == part * requests + i, ref[i], block)
    info_ref[...] = block

    pl.semaphore_wait(barrier, len(near) + len(others))

    def opposite(n):
        return n ^ 1

    infos = [
        remote(info_ref, told_ref.at[opposite(n)], info_send.at[n], info_recv.at[opposite(n)], near[n])
        for n in range(4)
    ]
    for copy in infos:
        copy.start()

    def route(kind):
        if kind == TWIN:
            return twin, 1, 1 - core, chip
        way = kind - 1
        there = paired(chip, way)
        return 2 * there + way, 2 + lax.rem(core + way, 2), way, there

    weights = []
    for kind in (1, 2, TWIN):
        index, source, way, there = route(kind)
        for part, block in enumerate((there, paired(there, 1 - way))):
            weights.append(
                remote(
                    proj_hbm.at[:, columns(block)],
                    weight_ref.at[source, :, pl.ds(part * 2 * width, 2 * width)],
                    weight_send.at[kind, part],
                    weight_recv.at[source - 1, part],
                    (worker, index),
                )
            )
    got_weights = [
        remote(
            proj_hbm.at[:, columns(chip)],
            weight_ref.at[source, :, pl.ds(part * 2 * width, 2 * width)],
            weight_send.at[source - 1, part],
            weight_recv.at[source - 1, part],
            (worker, twin),
        )
        for source in range(1, 4)
        for part in range(2)
    ]
    for copy in weights:
        copy.start()

    def hop(way, i):
        return remote(
            hop_out_ref.at[way, i], hop_in_ref.at[way, i], hop_send.at[way, i], hop_recv.at[way, i], near[2 + way]
        )

    def lend(way, i):
        return remote(
            lent_ref.at[way, i], borrowed_ref.at[way, i], lend_send.at[way, i], lend_recv.at[way, i], near[2 + way]
        )

    def send_end(way, i):
        return remote(
            sent_end_ref.at[i], got_end_ref.at[2 + way, i], end_send.at[2 + way, i], end_recv.at[2 + way, i], near[2 + way]
        )

    def pass_end(way, i):
        return remote(
            got_end_ref.at[2 + way, i], got_end_ref.at[way, i], end_send.at[way, i], end_recv.at[way, i], near[2 + way]
        )

    def send_normed(kind, i):
        index, source, way, _ = route(kind)
        return remote(
            normed_ref.at[i, rows(way)],
            gathered_ref.at[i, source - 1],
            normed_send.at[kind, i],
            normed_recv.at[source - 1, i],
            (worker, index),
        )

    def get_normed(source, i):
        return remote(
            normed_ref.at[i, rows(core)],
            gathered_ref.at[i, source - 1],
            normed_send.at[source - 1, i],
            normed_recv.at[source - 1, i],
            (worker, twin),
        )

    def send_partial(i, c):
        return remote(
            passed_ref.at[i, c],
            got_ref.at[i, rows(core)],
            partial_send.at[i, c],
            partial_recv.at[i, core],
            (worker, 2 * beyond + c),
        )

    def get_partial(i, c):
        return remote(
            passed_ref.at[i, c], got_ref.at[i, rows(c)], partial_send.at[i, c], partial_recv.at[i, c], (worker, twin)
        )

    def swap(i):
        return remote(lent_sum_ref.at[i], twin_sum_ref.at[i], swap_send.at[i], swap_recv.at[i], (worker, twin))

    def wanted(n, i):
        return cache_ref[jnp.clip(told_smem[n, 0, requests + i], 0, slots - 1)].astype(jnp.bfloat16)

    def answer():
        for n in range(4):
            remote(info_ref, told_ref.at[n], info_send.at[n], info_recv.at[n], near[n]).wait_recv()
        fetch = pltpu.make_async_copy(told_ref, told_smem, told_sem)
        fetch.start()
        fetch.wait()
        loads[6].wait()
        @pl.loop(0, requests)
        def _(i):
            for way in range(2):
                hop_out_ref[way, i] = wanted(way, i)
                hop(way, i).start()

    def merge(i):
        for way in range(2):
            hop(way, i).wait_recv()
            mine = told_smem[2 + way, 0, i] == worker
            lent_ref[way, i] = jnp.where(mine, wanted(2 + way, i), hop_in_ref[way, i])
            lend(way, i).start()

    def complete(i):
        for way in range(2):
            lend(way, i).wait_recv()
        move = lax.rem(owner_ref[i] - worker + workers + REACH, workers) - REACH
        node = jnp.clip(node_ref[i], 0, slots - 1)
        cached = prefix_ref[i] > 0
        starts = []
        for h in range(heads):
            start = cache_ref[node, h].astype(jnp.bfloat16)
            start = jnp.where(move < 0, borrowed_ref[1, i, h], start)
            start = jnp.where(move > 0, borrowed_ref[0, i, h], start)
            starts.append(jnp.where(cached, start, jnp.zeros_like(start)))
        slots_here = [i * heads + h for h in range(heads)]
        normed, ends = finish(slots_here, starts, zhi_ref, zlo_ref, base_ref, gain_gate_ref)
        for h in range(heads):
            normed_ref[i, :, h * DV : (h + 1) * DV] = normed[h]
            sent_end_ref[i, h] = ends[h].astype(jnp.bfloat16)
        for kind in (1, 2, TWIN):
            send_normed(kind, i).start()
        for way in range(2):
            send_end(way, i).start()

    def relay(i):
        for way in range(2):
            send_end(way, i).wait_recv()
            pass_end(way, i).start()

    def project(i):
        total = dot1(normed_ref[i, rows(core)], weight_ref[0])
        for source in range(1, 4):
            get_normed(source, i).wait_recv()
            total = total + dot1(gathered_ref[i, source - 1], weight_ref[source])
        for c in range(2):
            passed_ref[i, c] = total[:, (2 + c) * width : (3 + c) * width].astype(jnp.bfloat16)
            send_partial(i, c).start()
        left, right = total[:, :width], total[:, width : 2 * width]
        lent_sum_ref[i] = jnp.where(core == 0, right, left).astype(jnp.bfloat16)
        swap(i).start()
        kept_ref[i] = jnp.where(core == 0, left, right)

    def add(i):
        swap(i).wait_recv()
        for c in range(2):
            get_partial(i, c).wait_recv()
        for sums, c in ((kept_ref, core), (twin_sum_ref, 1 - core)):
            mixed_ref[i, rows(c)] = (sums[i].astype(jnp.float32) + got_ref[i, rows(c)].astype(jnp.float32)).astype(
                jnp.bfloat16
            )

    for load in loads[:6] + loads[7:]:
        load.wait()

    def ready(rs, between):
        prepare(
            rs, between, q_ref, k_ref, v_ref, gate_ref, decay_ref, rate_ref, gain_ref, zhi_ref, zlo_ref, base_ref, gain_gate_ref
        )

    @pl.loop(0, requests // 2)
    def _(pair):
        def between():
            pl.when(pair == 0)(answer)

            @pl.when(pair == 1)
            def _():
                pl.loop(0, 2)(merge)

        ready([2 * pair, 2 * pair + 1], between)

    pl.loop(2, requests)(merge)
    pl.loop(0, requests)(complete)
    for load in weight_loads:
        load.wait()
    for copy in got_weights:
        copy.wait_recv()

    @pl.loop(0, requests)
    def _(i):
        project(i)
        relay(i)

    pl.loop(0, requests)(add)
    for i in range(requests):
        for way in range(2):
            pass_end(way, i).wait_recv()
    for target in range(requests):
        row = worker * requests + target
        mine, theirs = jnp.int32(0), jnp.int32(0)
        kept = jnp.bool_(False)
        for i in range(requests):
            here = slot_ref[i] == row
            kept = kept | here
            mine = jnp.where(here, i, mine)
            for n in range(4):
                theirs = jnp.where(told_smem[opposite(n), 0, 3 * requests + i] == row, n * requests + i, theirs)
        end_ref[target] = jnp.where(
            kept, sent_end_ref[mine], got_end_ref[theirs // requests, theirs % requests]
        )

    for copy in infos + weights:
        copy.wait_send()
    for i in range(requests):
        for way in range(2):
            hop(way, i).wait_send()
            lend(way, i).wait_send()
            send_end(way, i).wait_send()
            pass_end(way, i).wait_send()
        for kind in range(3):
            send_normed(kind, i).wait_send()
        for c in range(2):
            send_partial(i, c).wait_send()
        swap(i).wait_send()


def store_kernel(mixed_ref, end_ref, mixed_hbm, end_hbm, wide_ref, mixed_sem, end_sem):
    requests = mixed_ref.shape[0]
    copies = [pltpu.make_async_copy(mixed_ref.at[i], mixed_hbm.at[i], mixed_sem.at[i]) for i in range(requests)]
    for copy in copies:
        copy.start()
    for i in range(requests):
        wide_ref[i] = end_ref[i].astype(jnp.float32)
        copies.append(pltpu.make_async_copy(wide_ref.at[i], end_hbm.at[i], end_sem.at[i]))
        copies[-1].start()
    for copy in copies:
        copy.wait()


def on_device(
    queries,
    key_heads,
    values_in,
    out_gate,
    log_decay,
    write_rate,
    cache_states,
    norm_gain,
    out_proj,
    hit_owner,
    hit_node,
    prefix_len,
    write_slot,
):
    requests, tokens = queries.shape[:2]
    heads = log_decay.shape[1]
    width = heads * DV
    state = cache_states.shape[1:]
    vmem = pl.BlockSpec(memory_space=pltpu.VMEM)
    anywhere = pl.BlockSpec(memory_space=pltpu.HBM)
    low, wide = jnp.bfloat16, jnp.float32
    dma = pltpu.SemaphoreType.DMA
    mixed, ends = pl.pallas_call(
        functools.partial(layer_kernel, lax.axis_size("worker")),
        out_shape=(
            pltpu.VMEM((requests, tokens, width), low),
            pltpu.VMEM((requests, *state), low),
        ),
        in_specs=[anywhere] * 13,
        out_specs=(vmem, vmem),
        scratch_shapes=[
            *[pltpu.SMEM((requests,), jnp.int32)] * 4,
            pltpu.VMEM((1, DV), wide),
            pltpu.VMEM(queries.shape, low),
            pltpu.VMEM(key_heads.shape, low),
            pltpu.VMEM(values_in.shape, low),
            pltpu.VMEM(out_gate.shape, low),
            pltpu.VMEM(log_decay.shape, wide),
            pltpu.VMEM(write_rate.shape, wide),
            pltpu.VMEM(cache_states.shape, wide),
            pltpu.VMEM((requests * heads, tokens + DK, DK), low),
            pltpu.VMEM((requests * heads, tokens + DK, DK), low),
            pltpu.VMEM((requests * heads, tokens + DK, DV), wide),
            pltpu.VMEM((requests * heads, tokens, DV), wide),
            pltpu.VMEM((8, 128), jnp.int32),
            pltpu.VMEM((4, 8, 128), jnp.int32),
            pltpu.SMEM((4, 8, 128), jnp.int32),
            pltpu.VMEM((2, requests, *state), low),
            pltpu.VMEM((2, requests, *state), low),
            pltpu.VMEM((2, requests, *state), low),
            pltpu.VMEM((2, requests, *state), low),
            pltpu.VMEM((requests, *state), low),
            pltpu.VMEM((4, requests, *state), low),
            pltpu.VMEM((4, width, 4 * width), low),
            pltpu.VMEM((requests, tokens, width), low),
            pltpu.VMEM((requests, 3, tokens // 2, width), low),
            pltpu.VMEM((requests, tokens // 2, width), wide),
            pltpu.VMEM((requests, 2, tokens // 2, width), low),
            pltpu.VMEM((requests, tokens, width), low),
            pltpu.VMEM((requests, tokens // 2, width), low),
            pltpu.VMEM((requests, tokens // 2, width), low),
            dma((4,)),
            dma((8,)),
            dma((2,)),
            dma,
            dma((4,)),
            dma((4,)),
            dma((2, requests)),
            dma((2, requests)),
            dma((2, requests)),
            dma((2, requests)),
            dma((4, requests)),
            dma((4, requests)),
            dma((3, 2)),
            dma((3, 2)),
            dma((3, requests)),
            dma((3, requests)),
            dma((requests, 2)),
            dma((requests, 2)),
            dma((requests,)),
            dma((requests,)),
        ],
        compiler_params=pltpu.CompilerParams(
            collective_id=0, has_side_effects=True, vmem_limit_bytes=48 * 1024 * 1024
        ),
        name="layer",
    )(
        *(
            pltpu.with_memory_space_constraint(x, pltpu.HBM)
            for x in (
                hit_owner,
                hit_node,
                prefix_len,
                write_slot,
                norm_gain[None],
                queries,
                key_heads,
                values_in,
                out_gate,
                log_decay,
                write_rate,
                cache_states,
                out_proj,
            )
        )
    )
    return pl.pallas_call(
        store_kernel,
        out_shape=(jax.ShapeDtypeStruct(mixed.shape, low), jax.ShapeDtypeStruct(ends.shape, wide)),
        in_specs=[vmem] * 2,
        out_specs=(anywhere, anywhere),
        scratch_shapes=[pltpu.VMEM(ends.shape, wide), dma((requests,)), dma((requests,))],
        compiler_params=pltpu.CompilerParams(vmem_limit_bytes=32 * 1024 * 1024),
        name="store",
    )(mixed, ends)


def solution(mesh):
    in_specs = (
        P("worker", None, "tensor"),
        P("worker", None, "tensor"),
        P("worker", None, "tensor"),
        P("worker", None, "tensor"),
        P("worker", "tensor", None),
        P("worker", "tensor", None),
        P("worker", "tensor", None, None),
        P(),
        P("tensor", None),
        P("worker"),
        P("worker"),
        P("worker"),
        P("worker"),
    )
    out_specs = (P("worker", None, "tensor"), P("worker", "tensor", None, None))
    return jax.shard_map(
        on_device, mesh=mesh, in_specs=in_specs, out_specs=out_specs, check_vma=False
    )
```
